32 devices in a mesh: tile: 8 (over z, y), head: 4 (over x, core).
Axes of the slice: x: 2, y: 2, z: 4, core: 2. Of those that a mesh axis runs over, the one named last changes fastest.
Arguments:
- query_slab: bfloat16 [32, 2, 32, 5120], P('tile', None, 'head'), may hold values from -30 to 30
- key_slab: bfloat16 [32, 2, 32, 5120], P('tile', None, 'head'), may hold values from -5 to 5
- value_slab: bfloat16 [32, 2, 32, 5120], P('tile', None, 'head'), may hold values from -5 to 5
- upstream: bfloat16 [2048, 5120], P('tile', 'head'), may hold values from -5 to 5
Outputs:
- attended: bfloat16 [2048, 5120], P('tile', 'head')
- query_grad: bfloat16 [2048, 5120], P('tile', 'head')
- key_grad: bfloat16 [2048, 5120], P('tile', 'head')
- value_grad: bfloat16 [2048, 5120], P('tile', 'head')
The draws below stay inside these ranges and needn't reach their ends.
All inputs are finite; a program needn't handle non-finite values.
Results may differ from the reference program's by a relative error of at most 0.012.
Values may be sent and summed in bfloat16 or wider, within the bound.
A program may use at most 128 MiB of HBM per device.

```python
import jax
import jax.numpy as jnp
from jax import lax

HEADS = 40
HEAD_DIM = 128
FRAMES = 8
FRAME_W = 32
TILE_ROWS = 1
FRAME_H = 8
TOKENS = 2048
N_TILE = 8


def draw_query_slab(key, part):
    shape = (FRAMES * 4, FRAME_H // 4, FRAME_W, HEADS * HEAD_DIM)
    key = jax.random.fold_in(key, 1)
    return jnp.clip(jax.random.normal(key, shape), -5.0, 5.0).astype(jnp.bfloat16)


def draw_key_slab(key, part):
    shape = (FRAMES * 4, FRAME_H // 4, FRAME_W, HEADS * HEAD_DIM)
    key = jax.random.fold_in(key, 2)
    return jnp.clip(jax.random.normal(key, shape), -5.0, 5.0).astype(jnp.bfloat16)


def level_of(key, shape, shards, smallest, top_value):
    gain = 1.0
    for axis_at, parts in shards:
        steps = jax.random.uniform(jax.random.fold_in(jax.random.fold_in(key, 6), axis_at), (parts,), jnp.float32, smallest / len(shards), top_value / len(shards))
        gain = gain * jnp.repeat(jnp.exp(steps), shape[axis_at] // parts).reshape((-1,) + (1,) * (len(shape) - 1 - axis_at))
    return gain


def gaussian(key, shape, deviation, bound, split=(), held_as=jnp.bfloat16):
    factor_of = level_of(key, shape, split, -0.22, 0.18) if split else 1.0
    entries = jax.random.normal(key, shape, jnp.float32) * deviation * factor_of
    return jnp.minimum(jnp.maximum(entries, -bound), bound).astype(held_as)


def setup_inputs(seed: int = 0) -> dict:
    seeds = jax.random.split(jax.random.key(seed), 5)
    query_slab = draw_query_slab(jax.random.fold_in(seeds[4], 71), 0)
    key_slab = draw_key_slab(jax.random.fold_in(seeds[4], 71), 0)
    value_slab = gaussian(seeds[2], (4 * FRAMES, FRAME_H // 4, FRAME_W, HEADS * HEAD_DIM), 1.0, 5.0, ((0, 8), (2, 4)))
    upstream = gaussian(seeds[3], (TOKENS, HEADS * HEAD_DIM), 1.0, 5.0, ((0, 8), (1, 4)))
    return {"query_slab": query_slab, "key_slab": key_slab, "value_slab": value_slab, "upstream": upstream}


masked_score = -1.0e30


def to_tiles(grid, tile_rows, tile_cols):
    features = grid.shape[-1]
    shaped = grid.reshape(FRAMES, tile_rows, 4, tile_cols, 4, features)
    return shaped.transpose(1, 3, 0, 2, 4, 5).reshape(tile_rows, tile_cols, FRAMES * 16, features)


def from_tiles(tiles):
    tile_rows = tiles.shape[0]
    tile_cols = tiles.shape[1]
    features = tiles.shape[-1]
    shaped = tiles.reshape(tile_rows, tile_cols, FRAMES, 4, 4, features)
    return shaped.transpose(2, 0, 3, 1, 4, 5).reshape(FRAMES * tile_rows * tile_cols * 16, features)


def window_keys(nearby, tile_rows, tile_cols):
    features = nearby.shape[-1]
    shaped = nearby.reshape(2, FRAMES, tile_rows + 2, 4, tile_cols + 2, 4, features)
    pieces = [shaped[:, :, row_step:row_step + tile_rows, :, col_step:col_step + tile_cols] for row_step in range(3) for col_step in range(3)]
    stacked = jnp.stack(pieces, axis=1)
    ordered = stacked.transpose(0, 3, 5, 1, 2, 4, 6, 7)
    return ordered.reshape(2, tile_rows, tile_cols, 144 * FRAMES, features)


def fold_keys(window, tile_rows, tile_cols):
    features = window.shape[-1]
    portions = window.reshape(tile_rows, tile_cols, 3, 3, FRAMES, 4, 4, features)
    accumulated = jnp.zeros((FRAMES, tile_rows + 2, 4, tile_cols + 2, 4, features), jnp.float32)
    for row_step in range(3):
        for col_step in range(3):
            portion = portions[:, :, row_step, col_step].transpose(2, 0, 3, 1, 4, 5)
            accumulated = accumulated.at[:, row_step:row_step + tile_rows, :, col_step:col_step + tile_cols].add(portion)
    return accumulated.reshape(FRAMES, 4 * (tile_rows + 2), 4 * (tile_cols + 2), features)


def key_mask(tile_rows, tile_cols, row_first, col_first, rows_all, cols_all):
    row_index = jnp.arange(tile_rows, dtype=jnp.int32)[:, None, None, None]
    col_index = jnp.arange(tile_cols, dtype=jnp.int32)[None, :, None, None]
    row_steps = jnp.arange(3, dtype=jnp.int32)[None, None, :, None]
    col_steps = jnp.arange(3, dtype=jnp.int32)[None, None, None, :]
    row_place = row_first + row_index + row_steps - 1
    col_place = col_first + col_index + col_steps - 1
    usable = (row_place >= 0) & (row_place < rows_all) & (col_place >= 0) & (col_place < cols_all)
    spread = jnp.broadcast_to(usable[..., None], (tile_rows, tile_cols, 3, 3, FRAMES * 16))
    return spread.reshape(tile_rows, tile_cols, 144 * FRAMES)


def attend(query_blocks, key_window, value_window, grad_blocks, usable):
    tile_rows, pair_count, query_count, features = query_blocks.shape
    head_count = features // HEAD_DIM
    key_count = key_window.shape[2]
    best = lax.Precision.HIGHEST
    query_heads = query_blocks.astype(jnp.float32).reshape(tile_rows, pair_count, query_count, head_count, HEAD_DIM)
    grad_heads = grad_blocks.astype(jnp.float32).reshape(tile_rows, pair_count, query_count, head_count, HEAD_DIM)
    key_heads = key_window.astype(jnp.float32).reshape(tile_rows, pair_count, key_count, head_count, HEAD_DIM)
    value_heads = value_window.astype(jnp.float32).reshape(tile_rows, pair_count, key_count, head_count, HEAD_DIM)
    scaling = HEAD_DIM ** -0.5
    scores = jnp.einsum("rcqhd,rckhd->rchqk", query_heads, key_heads, precision=best) * scaling
    scores = jnp.where(usable[:, :, None, None, :], scores, masked_score)
    highest = jnp.max(scores, axis=-1, keepdims=True)
    raised = jnp.exp(scores - highest)
    weights = raised / jnp.sum(raised, axis=-1, keepdims=True)
    weights_low = lax.optimization_barrier(weights.astype(jnp.bfloat16)).astype(jnp.float32)
    mixed = jnp.einsum("rchqk,rckhd->rcqhd", weights_low, value_heads, precision=best)
    offsets = jnp.sum(grad_heads * mixed, axis=-1).transpose(0, 1, 3, 2)
    weight_grad = jnp.einsum("rcqhd,rckhd->rchqk", grad_heads, value_heads, precision=best)
    score_grad = weights * (weight_grad - offsets[..., None])
    score_low = lax.optimization_barrier(score_grad.astype(jnp.bfloat16)).astype(jnp.float32)
    query_grad = jnp.einsum("rchqk,rckhd->rcqhd", score_low, key_heads, precision=best) * scaling
    key_terms = jnp.einsum("rchqk,rcqhd->rckhd", score_low, query_heads, precision=best) * scaling
    value_terms = jnp.einsum("rchqk,rcqhd->rckhd", weights_low, grad_heads, precision=best)
    return (mixed.reshape(tile_rows, pair_count, query_count, features),
            query_grad.reshape(tile_rows, pair_count, query_count, features),
            key_terms.reshape(tile_rows, pair_count, key_count, features),
            value_terms.reshape(tile_rows, pair_count, key_count, features))


def reference(query_slab, key_slab, value_slab, upstream):
    features = HEADS * HEAD_DIM
    tile_cols = FRAME_W // 16
    band_width = 4 * tile_cols
    line_count = 4 * TILE_ROWS
    rows_all = FRAME_H // 4

    def to_grid(slab):
        shaped = slab.reshape(FRAMES, 4, rows_all, FRAME_W, features).transpose(0, 2, 1, 3, 4)
        return shaped.reshape(FRAMES, FRAME_H, FRAME_W, features)

    query_grid = to_grid(query_slab)
    pair_grid = jnp.stack((to_grid(key_slab), to_grid(value_slab)))
    padded = jnp.pad(pair_grid, ((0, 0), (0, 0), (4, 4), (4, 4), (0, 0)))
    grad_owned = upstream.reshape(N_TILE, FRAMES, line_count, band_width, features)

    def one_owner(owner_index):
        row_group = owner_index // 4
        col_group = owner_index % 4
        zero = jnp.zeros((), jnp.int32)
        row_first = row_group * line_count
        col_first = col_group * band_width
        owned_query = lax.dynamic_slice(query_grid, (zero, row_first, col_first, zero), (FRAMES, line_count, band_width, features))
        nearby = lax.dynamic_slice(padded, (zero, zero, row_first, col_first, zero), (2, FRAMES, line_count + 8, band_width + 8, features))
        windows = window_keys(nearby, TILE_ROWS, tile_cols)
        usable = key_mask(TILE_ROWS, tile_cols, row_group * TILE_ROWS, col_group * tile_cols, rows_all, 4 * tile_cols)
        grad_rows = lax.dynamic_index_in_dim(grad_owned, owner_index, 0, keepdims=False)
        mixed, query_grad, key_terms, value_terms = attend(to_tiles(owned_query, TILE_ROWS, tile_cols), windows[0], windows[1], to_tiles(grad_rows, TILE_ROWS, tile_cols), usable)
        extended = jnp.stack((fold_keys(key_terms, TILE_ROWS, tile_cols), fold_keys(value_terms, TILE_ROWS, tile_cols)))
        middle = extended[:, :, 4:4 + line_count]
        return (from_tiles(mixed).astype(jnp.bfloat16), from_tiles(query_grad).astype(jnp.bfloat16), middle,
                extended[:, :, 0:4].astype(jnp.bfloat16), extended[:, :, line_count + 4:].astype(jnp.bfloat16))

    attended, query_grad, middle, top_bands, bottom_bands = lax.map(one_owner, jnp.arange(N_TILE, dtype=jnp.int32))
    empty_rows = jnp.zeros_like(top_bands[:4])
    from_above = jnp.concatenate((empty_rows, bottom_bands[:-4]), axis=0).astype(jnp.float32)
    from_below = jnp.concatenate((top_bands[4:], empty_rows), axis=0).astype(jnp.float32)
    incoming = jnp.pad(from_above, ((0, 0), (0, 0), (0, 0), (0, line_count - 4), (0, 0), (0, 0)))
    incoming = incoming + jnp.pad(from_below, ((0, 0), (0, 0), (0, 0), (line_count - 4, 0), (0, 0), (0, 0)))
    rowed = middle + incoming
    left_bands = rowed[:, :, :, :, 0:4].astype(jnp.bfloat16)
    right_bands = rowed[:, :, :, :, band_width + 4:].astype(jnp.bfloat16)
    col_groups = (jnp.arange(N_TILE, dtype=jnp.int32) % 4)[:, None, None, None, None, None]
    empty_one = jnp.zeros_like(left_bands[:1])
    from_left = jnp.where(col_groups > 0, jnp.concatenate((empty_one, right_bands[:-1]), axis=0), jnp.zeros_like(right_bands)).astype(jnp.float32)
    from_right = jnp.where(col_groups < 3, jnp.concatenate((left_bands[1:], empty_one), axis=0), jnp.zeros_like(left_bands)).astype(jnp.float32)
    summed = rowed[:, :, :, :, 4:band_width + 4]
    summed = summed + jnp.pad(from_left, ((0, 0), (0, 0), (0, 0), (0, 0), (0, band_width - 4), (0, 0)))
    summed = summed + jnp.pad(from_right, ((0, 0), (0, 0), (0, 0), (0, 0), (band_width - 4, 0), (0, 0)))
    summed = summed.astype(jnp.bfloat16)
    key_grad = summed[:, 0].reshape(TOKENS, features)
    value_grad = summed[:, 1].reshape(TOKENS, features)
    return (attended.reshape(TOKENS, features), query_grad.reshape(TOKENS, features), key_grad, value_grad)
```

```python
import math

import jax
import jax.numpy as jnp
from jax import lax
from jax.experimental import pallas as pl
from jax.experimental.pallas import tpu as pltpu
from jax.sharding import PartitionSpec as P

HEAD_DIM = 128
FRAMES = 8
FRAME_W = 32
MESH = pl.DeviceIdType.MESH


masked_score = -1e30


def from_behind(value, axis, steps):
    count = lax.axis_size(axis)
    leading, last = (max(0, -steps), min(count, count - steps))
    return lax.ppermute(value, axis, [(source, source + steps) for source in range(leading, last)])


def to_tiles(grid, tile_rows, tile_cols):
    features = grid.shape[-1]
    shaped = grid.reshape(FRAMES, tile_rows, 4, tile_cols, 4, features)
    return shaped.transpose(1, 3, 0, 2, 4, 5).reshape(tile_rows, tile_cols, FRAMES * 16, features)


def from_tiles(tiles):
    tile_rows = tiles.shape[0]
    tile_cols = tiles.shape[1]
    features = tiles.shape[-1]
    shaped = tiles.reshape(tile_rows, tile_cols, FRAMES, 4, 4, features)
    return shaped.transpose(2, 0, 3, 1, 4, 5).reshape(FRAMES * tile_rows * tile_cols * 16, features)


def window_keys(nearby, tile_rows, tile_cols):
    features = nearby.shape[-1]
    shaped = nearby.reshape(2, FRAMES, tile_rows + 2, 4, tile_cols + 2, 4, features)
    pieces = [
        shaped[:, :, row_step : row_step + tile_rows, :, col_step : col_step + tile_cols]
        for row_step in range(3)
        for col_step in range(3)
    ]
    stacked = jnp.stack(pieces, axis=1)
    ordered = stacked.transpose(0, 3, 5, 1, 2, 4, 6, 7)
    return ordered.reshape(2, tile_rows, tile_cols, 144 * FRAMES, features)


def fold_keys(window, tile_rows, tile_cols):
    features = window.shape[-1]
    portions = window.reshape(tile_rows, tile_cols, 3, 3, FRAMES, 4, 4, features)
    accumulated = jnp.zeros((FRAMES, tile_rows + 2, 4, tile_cols + 2, 4, features), jnp.float32)
    for row_step in range(3):
        for col_step in range(3):
            portion = portions[:, :, row_step, col_step].transpose(2, 0, 3, 1, 4, 5)
            accumulated = accumulated.at[
                :, row_step : row_step + tile_rows, :, col_step : col_step + tile_cols
            ].add(portion)
    return accumulated.reshape(FRAMES, 4 * (tile_rows + 2), 4 * (tile_cols + 2), features)


def key_mask(tile_rows, tile_cols, row_first, col_first, rows_all, cols_all):
    row_index = jnp.arange(tile_rows, dtype=jnp.int32)[:, None, None, None]
    col_index = jnp.arange(tile_cols, dtype=jnp.int32)[None, :, None, None]
    row_steps = jnp.arange(3, dtype=jnp.int32)[None, None, :, None]
    col_steps = jnp.arange(3, dtype=jnp.int32)[None, None, None, :]
    row_place = row_first + row_index + row_steps - 1
    col_place = col_first + col_index + col_steps - 1
    usable = (row_place >= 0) & (row_place < rows_all) & (col_place >= 0) & (col_place < cols_all)
    spread = jnp.broadcast_to(usable[..., None], (tile_rows, tile_cols, 3, 3, FRAMES * 16))
    return spread.reshape(tile_rows, tile_cols, 144 * FRAMES)


def attend(query_blocks, key_window, value_window, grad_blocks, usable):
    tile_rows, pair_count, query_count, features = query_blocks.shape
    head_count = features // HEAD_DIM
    key_count = key_window.shape[2]
    query_heads = query_blocks.reshape(tile_rows, pair_count, query_count, head_count, HEAD_DIM)
    grad_heads = grad_blocks.reshape(tile_rows, pair_count, query_count, head_count, HEAD_DIM)
    key_heads = key_window.reshape(tile_rows, pair_count, key_count, head_count, HEAD_DIM)
    value_heads = value_window.reshape(tile_rows, pair_count, key_count, head_count, HEAD_DIM)
    scaling = HEAD_DIM ** (-0.5)
    scores = (
        jnp.einsum("rcqhd,rckhd->rchqk", query_heads, key_heads, preferred_element_type=jnp.float32)
        * scaling
    )
    scores = jnp.where(usable[:, :, None, None, :], scores, masked_score)
    highest = jnp.max(scores, axis=-1, keepdims=True)
    raised = jnp.exp(scores - highest)
    weights = raised / jnp.sum(raised, axis=-1, keepdims=True)
    weights_low = weights.astype(jnp.bfloat16)
    mixed = jnp.einsum(
        "rchqk,rckhd->rcqhd", weights_low, value_heads, preferred_element_type=jnp.float32
    )
    offsets = jnp.sum(grad_heads.astype(jnp.float32) * mixed, axis=-1).transpose(0, 1, 3, 2)
    weight_grad = jnp.einsum(
        "rcqhd,rckhd->rchqk", grad_heads, value_heads, preferred_element_type=jnp.float32
    )
    score_grad = weights * (weight_grad - offsets[..., None])
    score_low = score_grad.astype(jnp.bfloat16)
    query_grad = (
        jnp.einsum("rchqk,rckhd->rcqhd", score_low, key_heads, preferred_element_type=jnp.float32)
        * scaling
    )
    key_terms = (
        jnp.einsum("rchqk,rcqhd->rckhd", score_low, query_heads, preferred_element_type=jnp.float32)
        * scaling
    )
    value_terms = jnp.einsum(
        "rchqk,rcqhd->rckhd", weights_low, grad_heads, preferred_element_type=jnp.float32
    )
    return (
        mixed.reshape(tile_rows, pair_count, query_count, features),
        query_grad.reshape(tile_rows, pair_count, query_count, features),
        key_terms.reshape(tile_rows, pair_count, key_count, features),
        value_terms.reshape(tile_rows, pair_count, key_count, features),
    )


def pass_keys(block, step):
    return from_behind(block, "tile", step)


def pass_terms(block, step):
    return from_behind(block, "tile", step)


def settle(received):
    rows_here = received.shape[-3]
    width_here = received.shape[-2]
    features = received.shape[-1]
    shaped = received.reshape(FRAMES, 4, rows_here, width_here, features).transpose(0, 2, 1, 3, 4)
    return shaped.reshape(FRAMES, 4 * rows_here, width_here, features)


def local(query_slab, key_slab, value_slab, upstream):
    query_rows, key_rows, value_rows = (
        lax.all_to_all(query_slab, "head", split_axis=3, concat_axis=2, tiled=True),
        lax.all_to_all(key_slab, "head", split_axis=3, concat_axis=2, tiled=True),
        lax.all_to_all(value_slab, "head", split_axis=3, concat_axis=2, tiled=True),
    )
    owner_count = lax.axis_size("tile")
    row_groups = owner_count // 4
    source_count = query_rows.shape[0]
    features = query_rows.shape[3]
    tile_rows = query_rows.shape[1] // row_groups
    tile_cols = FRAME_W // 16
    band_width = 4 * tile_cols
    line_count = 4 * tile_rows
    owner_index = lax.axis_index("tile")
    row_group = owner_index // 4
    col_group = owner_index % 4
    left_ok = col_group > 0
    right_ok = col_group < 3

    def to_owners(slab):
        shaped = slab.reshape(source_count, row_groups, tile_rows, 4, band_width, features)
        return shaped.transpose(1, 3, 0, 2, 4, 5).reshape(
            owner_count, source_count, tile_rows, band_width, features
        )

    query_got, key_got, value_got = (
        lax.all_to_all(to_owners(query_rows), "tile", split_axis=0, concat_axis=1, tiled=True),
        lax.all_to_all(to_owners(key_rows), "tile", split_axis=0, concat_axis=1, tiled=True),
        lax.all_to_all(to_owners(value_rows), "tile", split_axis=0, concat_axis=1, tiled=True),
    )
    owned_query = settle(query_got)
    owned_pair = jnp.stack((settle(key_got), settle(value_got)))
    from_left = pass_keys(owned_pair[:, :, :, band_width - 4 :], 1)
    from_right = pass_keys(owned_pair[:, :, :, 0:4], -1)
    from_left = jnp.where(left_ok, from_left, jnp.zeros_like(from_left))
    from_right = jnp.where(right_ok, from_right, jnp.zeros_like(from_right))
    wide_pair = jnp.concatenate((from_left, owned_pair, from_right), axis=3)
    from_above = pass_keys(wide_pair, 4)
    from_below = pass_keys(wide_pair, -4)
    nearby = jnp.concatenate((from_above, wide_pair, from_below), axis=2)
    query_tiles = to_tiles(owned_query, tile_rows, tile_cols)
    grad_tiles = to_tiles(
        upstream.reshape(FRAMES, line_count, band_width, features), tile_rows, tile_cols
    )
    usable = key_mask(
        tile_rows,
        tile_cols,
        row_group * tile_rows,
        col_group * tile_cols,
        row_groups * tile_rows,
        4 * tile_cols,
    )
    totals = jnp.zeros((2, FRAMES, line_count + 8, band_width + 8, features), jnp.float32)

    def one_column(totals, column):
        first_col = column * 4
        nearby_part = lax.dynamic_slice_in_dim(nearby, first_col, 12, 3)
        windows = window_keys(nearby_part, tile_rows, 1)
        query_part = lax.dynamic_slice_in_dim(query_tiles, column, 1, 1)
        grad_part = lax.dynamic_slice_in_dim(grad_tiles, column, 1, 1)
        usable_part = lax.dynamic_slice_in_dim(usable, column, 1, 1)
        mixed, query_grad, key_terms, value_terms = attend(
            query_part, windows[0], windows[1], grad_part, usable_part
        )
        folded = jnp.stack(
            (fold_keys(key_terms, tile_rows, 1), fold_keys(value_terms, tile_rows, 1))
        )
        current = lax.dynamic_slice_in_dim(totals, first_col, 12, 3)
        totals = lax.dynamic_update_slice_in_dim(totals, current + folded, first_col, 3)
        return (totals, (mixed[:, 0].astype(jnp.bfloat16), query_grad[:, 0].astype(jnp.bfloat16)))

    extended, (mixed, query_grad) = lax.scan(
        one_column, totals, jnp.arange(tile_cols, dtype=jnp.int32)
    )
    attended = from_tiles(jnp.swapaxes(mixed, 0, 1))
    query_out = from_tiles(jnp.swapaxes(query_grad, 0, 1))
    top_band = extended[:, :, 0:4].astype(jnp.bfloat16)
    bottom_band = extended[:, :, line_count + 4 :].astype(jnp.bfloat16)
    terms_below = pass_terms(top_band, -4).astype(jnp.float32)
    terms_above = pass_terms(bottom_band, 4).astype(jnp.float32)
    incoming = terms_above
    incoming = incoming + terms_below
    rowed = extended[:, :, 4 : line_count + 4] + incoming
    left_terms = rowed[:, :, :, 0:4].astype(jnp.bfloat16)
    right_terms = rowed[:, :, :, band_width + 4 :].astype(jnp.bfloat16)
    terms_right = pass_terms(left_terms, -1)
    terms_left = pass_terms(right_terms, 1)
    terms_right = jnp.where(right_ok, terms_right, jnp.zeros_like(terms_right)).astype(jnp.float32)
    terms_left = jnp.where(left_ok, terms_left, jnp.zeros_like(terms_left)).astype(jnp.float32)
    summed = rowed[:, :, :, 4 : band_width + 4]
    summed = summed + jnp.pad(terms_left, ((0, 0), (0, 0), (0, 0), (0, band_width - 4), (0, 0)))
    summed = summed + jnp.pad(terms_right, ((0, 0), (0, 0), (0, 0), (band_width - 4, 0), (0, 0)))
    summed = summed.astype(jnp.bfloat16)
    key_grad = summed[0].reshape(-1, features)
    value_grad = summed[1].reshape(-1, features)
    return (attended, query_out, key_grad, value_grad)


SLOTS = 14


def fast_kernel(send_ref, up_ref, out_ref, qkv, gbuf, obuf, acc, landed, rims,
                main_send, main_recv, ext_send, ext_recv, left_send, left_recv, right_send, right_recv,
                up_send, up_recv, upx_send, upx_recv, out_send, out_recv, outx_send, outx_recv,
                rim_send, rim_recv):
    tile = lax.axis_index("tile")
    head = lax.axis_index("head")
    me = tile * 4 + head
    row_half = tile // 4
    col = tile % 4

    barrier = pltpu.get_barrier_semaphore()

    def greet(step, carry):
        other = (me + step) % 32
        pl.semaphore_signal(barrier, inc=1, device_id=(other // 4, other % 4), device_id_type=MESH)
        return carry

    lax.fori_loop(1, 32, greet, 0)
    pl.semaphore_wait(barrier, 31)

    def push(src, dst, send_sem, recv_sem, to_tile, to_head):
        return pltpu.make_async_remote_copy(
            src_ref=src, dst_ref=dst, send_sem=send_sem, recv_sem=recv_sem,
            device_id=(to_tile, to_head), device_id_type=MESH)

    def landing(dst, recv_sem):
        return pltpu.make_async_copy(dst, dst, recv_sem)

    def main_copy(other):
        to_tile, to_head = other // 4, other % 4
        src = send_ref.at[to_head * 10 + to_tile]
        dst = qkv.at[:, pl.ds(1 + 2 * head, 2), tile]
        return push(src, dst, main_send.at[other], main_recv.at[me], to_tile, to_head)

    def main_start(step, carry):
        main_copy((me + step) % 32).start()
        return carry

    lax.fori_loop(1, 32, main_start, 0)
    pltpu.make_async_copy(send_ref.at[head * 10 + tile], qkv.at[:, pl.ds(1 + 2 * head, 2), tile],
                          main_recv.at[me]).start()

    rows = pl.ds(16 * row_half, 16)

    def up_copy(other):
        return push(up_ref.at[other], gbuf.at[pl.ds(1 + 2 * col, 2), :, rows],
                    up_send.at[other], up_recv.at[tile], other, head)

    def up_start(step, carry):
        up_copy((tile + step) % 8).start()
        return carry

    lax.fori_loop(1, 8, up_start, 0)
    pltpu.make_async_copy(up_ref.at[tile], gbuf.at[pl.ds(1 + 2 * col, 2), :, rows], up_recv.at[tile]).start()

    def upx_copy(extra):
        return push(up_ref.at[8 + extra], gbuf.at[pl.ds(11, 2), :, rows],
                    upx_send.at[extra], upx_recv.at[row_half], 4 * extra + col, head)

    for extra in range(2):
        @pl.when(row_half == extra)
        def _(extra=extra):
            pltpu.make_async_copy(up_ref.at[8 + extra], gbuf.at[pl.ds(11, 2), :, rows],
                                  upx_recv.at[row_half]).start()

        @pl.when(row_half != extra)
        def _(extra=extra):
            upx_copy(extra).start()

    def ext_parts(which):
        to_head, extra = which // 2, which % 2
        return to_head, extra, to_head * 10 + 8 + extra

    def ext_copy(which):
        to_head, extra, source = ext_parts(which)
        return push(send_ref.at[source], qkv.at[:, pl.ds(11, 2), tile],
                    ext_send.at[which], ext_recv.at[tile], 4 * extra + head, to_head)

    def ext_is_own(which):
        to_head, extra, source = ext_parts(which)
        return (4 * extra + head) * 4 + to_head == me

    def left_copy(which):
        to_head, extra, source = ext_parts(which)
        return push(send_ref.at[source, pl.ds(1, 2), 1], qkv.at[pl.ds(1, 2), 10, tile],
                    left_send.at[which], left_recv.at[tile], 4 * extra + head + 1, to_head)

    def left_is_own(which):
        to_head, extra, source = ext_parts(which)
        return (4 * extra + head + 1) * 4 + to_head == me

    def right_copy(which):
        to_head, extra, source = ext_parts(which)
        return push(send_ref.at[source, pl.ds(1, 2), 0], qkv.at[pl.ds(1, 2), 13, tile],
                    right_send.at[which], right_recv.at[tile], 4 * extra + head - 1, to_head)

    def right_is_own(which):
        to_head, extra, source = ext_parts(which)
        return (4 * extra + head - 1) * 4 + to_head == me

    def ext_start(which, carry):
        to_head, extra, source = ext_parts(which)

        @pl.when(ext_is_own(which))
        def _():
            pltpu.make_async_copy(send_ref.at[source], qkv.at[:, pl.ds(11, 2), tile], ext_recv.at[tile]).start()

        @pl.when(jnp.logical_not(ext_is_own(which)))
        def _():
            ext_copy(which).start()

        @pl.when(head < 3)
        def _():
            @pl.when(left_is_own(which))
            def _():
                pltpu.make_async_copy(send_ref.at[source, pl.ds(1, 2), 1], qkv.at[pl.ds(1, 2), 10, tile],
                                      left_recv.at[tile]).start()

            @pl.when(jnp.logical_not(left_is_own(which)))
            def _():
                left_copy(which).start()

        @pl.when(head > 0)
        def _():
            @pl.when(right_is_own(which))
            def _():
                pltpu.make_async_copy(send_ref.at[source, pl.ds(1, 2), 0], qkv.at[pl.ds(1, 2), 13, tile],
                                      right_recv.at[tile]).start()

            @pl.when(jnp.logical_not(right_is_own(which)))
            def _():
                right_copy(which).start()

        return carry

    lax.fori_loop(0, 8, ext_start, 0)

    blank = jnp.zeros((FRAMES, 32, HEAD_DIM), jnp.bfloat16)
    for part in (1, 2):
        qkv[part, 0] = blank
        qkv[part, 9] = blank

        @pl.when(col == 0)
        def _(part=part):
            qkv[part, 10] = blank

        @pl.when(col == 3)
        def _(part=part):
            qkv[part, 13] = blank

    acc[...] = jnp.zeros_like(acc)

    def main_arrive(other, carry):
        landing(qkv.at[:, pl.ds(1 + 2 * (other % 4), 2), other // 4], main_recv.at[other]).wait()
        return carry

    lax.fori_loop(0, 32, main_arrive, 0)

    def up_arrive(other, carry):
        landing(gbuf.at[pl.ds(1 + 2 * (other % 4), 2), :, pl.ds(16 * (other // 4), 16)], up_recv.at[other]).wait()
        return carry

    lax.fori_loop(0, 8, up_arrive, 0)
    for half in range(2):
        landing(gbuf.at[pl.ds(11, 2), :, pl.ds(16 * half, 16)], upx_recv.at[half]).wait()

    def ext_arrive(frame, carry):
        landing(qkv.at[:, pl.ds(11, 2), frame], ext_recv.at[frame]).wait()

        @pl.when(col > 0)
        def _():
            landing(qkv.at[pl.ds(1, 2), 10, frame], left_recv.at[frame]).wait()

        @pl.when(col < 3)
        def _():
            landing(qkv.at[pl.ds(1, 2), 13, frame], right_recv.at[frame]).wait()

        return carry

    lax.fori_loop(0, 8, ext_arrive, 0)

    scaling = HEAD_DIM ** (-0.5)
    key_at = lax.broadcasted_iota(jnp.int32, (768, 1), 0)

    def one_tile(job, carry):
        first = job + 2 * (job // 8)
        low = jnp.where((job == 0) | ((job == 8) & (col == 0)), 256, 0)
        high = jnp.where((job == 7) | ((job == 9) & (col == 3)), 512, 768)
        usable = (key_at >= low) & (key_at < high)
        bias = jnp.where(usable, 0.0, -1e30)
        query = qkv[0, first + 1].reshape(256, HEAD_DIM)
        grad = gbuf[first + 1].reshape(256, HEAD_DIM)
        keys = qkv[1, pl.ds(first, 3)].reshape(768, HEAD_DIM)
        values = qkv[2, pl.ds(first, 3)].reshape(768, HEAD_DIM)
        scores = lax.dot_general(keys, query, (((1,), (1,)), ((), ())), preferred_element_type=jnp.float32)
        scores = scores * (scaling * math.log2(math.e)) + bias
        highest = jnp.max(scores, axis=0, keepdims=True)
        raised = jnp.exp2(scores - highest)
        weights = raised * (1.0 / jnp.sum(raised, axis=0, keepdims=True))
        weights_low = weights.astype(jnp.bfloat16)
        mixed = lax.dot_general(values, weights_low, (((0,), (0,)), ((), ())), preferred_element_type=jnp.float32)
        grad_across = grad.astype(jnp.float32).T
        offsets = jnp.sum(grad_across * mixed, axis=0, keepdims=True)
        weight_grad = lax.dot_general(values, grad, (((1,), (1,)), ((), ())), preferred_element_type=jnp.float32)
        score_low = (weights * (weight_grad - offsets)).astype(jnp.bfloat16)
        query_grad = lax.dot_general(keys, score_low, (((0,), (0,)), ((), ())), preferred_element_type=jnp.float32)
        obuf[0, first + 1] = mixed.T.astype(jnp.bfloat16).reshape(FRAMES, 32, HEAD_DIM)
        obuf[1, first + 1] = (query_grad * scaling).T.astype(jnp.bfloat16).reshape(FRAMES, 32, HEAD_DIM)
        key_terms = lax.dot_general(score_low, query, (((1,), (0,)), ((), ())), preferred_element_type=jnp.float32)
        value_terms = lax.dot_general(weights_low, grad, (((1,), (0,)), ((), ())), preferred_element_type=jnp.float32)
        acc[0, pl.ds(first, 3)] += (key_terms * scaling).reshape(3, 256, HEAD_DIM)
        acc[1, pl.ds(first, 3)] += value_terms.reshape(3, 256, HEAD_DIM)
        return carry

    lax.fori_loop(0, 10, one_tile, 0)

    def settle_slot(slot, carry):
        for part in range(2):
            obuf[2 + part, slot] = acc[part, slot].astype(jnp.bfloat16).reshape(FRAMES, 32, HEAD_DIM)
        return carry

    lax.fori_loop(1, SLOTS, settle_slot, 0)

    def out_parts(other):
        return obuf.at[:, pl.ds(1 + 2 * (other % 4), 2), :, pl.ds(16 * (other // 4), 16)]

    def out_copy(other):
        return push(out_parts(other), landed.at[:, tile], out_send.at[other], out_recv.at[tile], other, head)

    def out_start(step, carry):
        out_copy((tile + step) % 8).start()
        return carry

    lax.fori_loop(1, 8, out_start, 0)
    pltpu.make_async_copy(out_parts(tile), landed.at[:, tile], out_recv.at[tile]).start()

    def outx_copy(half):
        return push(obuf.at[:, pl.ds(11, 2), :, pl.ds(16 * half, 16)], landed.at[:, 8 + row_half],
                    outx_send.at[half], outx_recv.at[row_half], 4 * half + col, head)

    def rim_copy(half, side):
        slot, step = ((13, 1), (10, -1))[side]
        return push(obuf.at[pl.ds(2, 2), slot, :, pl.ds(16 * half, 16)], rims.at[row_half, side],
                    rim_send.at[half, side], rim_recv.at[row_half, side], 4 * half + col + step, head)

    for half in range(2):
        @pl.when(row_half == half)
        def _(half=half):
            pltpu.make_async_copy(obuf.at[:, pl.ds(11, 2), :, pl.ds(16 * half, 16)], landed.at[:, 8 + row_half],
                                  outx_recv.at[row_half]).start()

        @pl.when(row_half != half)
        def _(half=half):
            outx_copy(half).start()

        @pl.when(col < 3)
        def _(half=half):
            rim_copy(half, 0).start()

        @pl.when(col > 0)
        def _(half=half):
            rim_copy(half, 1).start()

    for extra in range(2):
        @pl.when(col == 0)
        def _(extra=extra):
            rims[extra, 0] = jnp.zeros((2, FRAMES, 16, HEAD_DIM), jnp.bfloat16)

        @pl.when(col == 3)
        def _(extra=extra):
            rims[extra, 1] = jnp.zeros((2, FRAMES, 16, HEAD_DIM), jnp.bfloat16)

    def out_arrive(other, carry):
        landing(landed.at[:, other], out_recv.at[other]).wait()
        for part in range(4):
            out_ref[part, other] = landed[part, other]
        return carry

    lax.fori_loop(0, 8, out_arrive, 0)
    for extra in range(2):
        landing(landed.at[:, 8 + extra], outx_recv.at[extra]).wait()

        @pl.when(col > 0)
        def _(extra=extra):
            landing(rims.at[extra, 0], rim_recv.at[extra, 0]).wait()

        @pl.when(col < 3)
        def _(extra=extra):
            landing(rims.at[extra, 1], rim_recv.at[extra, 1]).wait()

        for part in range(2):
            out_ref[part, 8 + extra] = landed[part, 8 + extra]
            for side in range(2):
                total = landed[2 + part, 8 + extra, side].astype(jnp.float32)
                total = total + rims[extra, side, part].astype(jnp.float32)
                out_ref[2 + part, 8 + extra, side] = total.astype(jnp.bfloat16)

    def main_left(step, carry):
        main_copy((me + step) % 32).wait_send()
        return carry

    lax.fori_loop(1, 32, main_left, 0)

    def group_left(step, carry):
        up_copy((tile + step) % 8).wait_send()
        out_copy((tile + step) % 8).wait_send()
        return carry

    lax.fori_loop(1, 8, group_left, 0)

    def ext_left(which, carry):
        @pl.when(jnp.logical_not(ext_is_own(which)))
        def _():
            ext_copy(which).wait_send()

        @pl.when((head < 3) & jnp.logical_not(left_is_own(which)))
        def _():
            left_copy(which).wait_send()

        @pl.when((head > 0) & jnp.logical_not(right_is_own(which)))
        def _():
            right_copy(which).wait_send()

        return carry

    lax.fori_loop(0, 8, ext_left, 0)
    for half in range(2):
        @pl.when(row_half != half)
        def _(half=half):
            upx_copy(half).wait_send()
            outx_copy(half).wait_send()

        @pl.when(col < 3)
        def _(half=half):
            rim_copy(half, 0).wait_send()

        @pl.when(col > 0)
        def _(half=half):
            rim_copy(half, 1).wait_send()


def fast_local(query_slab, key_slab, value_slab, upstream):
    def by_head(slab):
        shaped = slab.reshape(4, 2, 2, 4, 40, HEAD_DIM).transpose(4, 2, 1, 0, 3, 5)
        return shaped.reshape(40, 2, 32, HEAD_DIM)

    send = jnp.stack((by_head(query_slab), by_head(key_slab), by_head(value_slab)), axis=1)
    up = upstream.reshape(FRAMES, 4, 2, 4, 10, HEAD_DIM).transpose(4, 2, 0, 1, 3, 5)
    up = up.reshape(10, 2, FRAMES, 16, HEAD_DIM)
    dma = pltpu.SemaphoreType.DMA
    out = pl.pallas_call(
        fast_kernel,
        out_shape=jax.ShapeDtypeStruct((4, 10, 2, FRAMES, 16, HEAD_DIM), jnp.bfloat16),
        in_specs=[pl.BlockSpec(memory_space=pltpu.VMEM)] * 2,
        out_specs=pl.BlockSpec(memory_space=pltpu.VMEM),
        scratch_shapes=[
            pltpu.VMEM((3, SLOTS, FRAMES, 32, HEAD_DIM), jnp.bfloat16),
            pltpu.VMEM((SLOTS, FRAMES, 32, HEAD_DIM), jnp.bfloat16),
            pltpu.VMEM((4, SLOTS, FRAMES, 32, HEAD_DIM), jnp.bfloat16),
            pltpu.VMEM((2, SLOTS, 256, HEAD_DIM), jnp.float32),
            pltpu.VMEM((4, 10, 2, FRAMES, 16, HEAD_DIM), jnp.bfloat16),
            pltpu.VMEM((2, 2, 2, FRAMES, 16, HEAD_DIM), jnp.bfloat16),
            dma((32,)), dma((32,)), dma((8,)), dma((8,)), dma((8,)), dma((8,)), dma((8,)), dma((8,)),
            dma((8,)), dma((8,)), dma((2,)), dma((2,)), dma((8,)), dma((8,)), dma((2,)), dma((2,)),
            dma((2, 2)), dma((2, 2)),
        ],
        compiler_params=pltpu.CompilerParams(
            collective_id=0, has_side_effects=True, vmem_limit_bytes=48 * 1024 * 1024
        ),
        cost_estimate=pl.CostEstimate(flops=3 * 10**9, bytes_accessed=8 * 10**6, transcendentals=2 * 10**6),
    )(send, up)
    out = out.reshape(4, 10, 2, FRAMES, 4, 4, HEAD_DIM).transpose(0, 3, 4, 2, 5, 1, 6).reshape(4, 256, 1280)
    return (out[0], out[1], out[2], out[3])


def solution(mesh):
    placed = (
        P("tile", None, "head", None),
        P("tile", None, "head", None),
        P("tile", None, "head", None),
        P("tile", "head"),
    )

    def chosen(query_slab, key_slab, value_slab, upstream):
        two_rows = query_slab.shape == (4, 2, 8, 40 * HEAD_DIM) and upstream.shape == (256, 10 * HEAD_DIM)
        body = fast_local if two_rows and mesh.shape["tile"] == 8 and mesh.shape["head"] == 4 else local
        return body(query_slab, key_slab, value_slab, upstream)

    return jax.shard_map(
        chosen,
        mesh=mesh,
        in_specs=placed,
        out_specs=(P("tile", "head"), P("tile", "head"), P("tile", "head"), P("tile", "head")),
        check_vma=False,
    )
```

```python
import math

import jax
import jax.numpy as jnp
from jax import lax
from jax.experimental import pallas as pl
from jax.experimental.pallas import tpu as pltpu
from jax.sharding import PartitionSpec as P

HEAD_DIM = 128
FRAMES = 8
FRAME_W = 32
MESH = pl.DeviceIdType.MESH


masked_score = -1e30


def from_behind(value, axis, steps):
    count = lax.axis_size(axis)
    leading, last = (max(0, -steps), min(count, count - steps))
    return lax.ppermute(value, axis, [(source, source + steps) for source in range(leading, last)])


def to_tiles(grid, tile_rows, tile_cols):
    features = grid.shape[-1]
    shaped = grid.reshape(FRAMES, tile_rows, 4, tile_cols, 4, features)
    return shaped.transpose(1, 3, 0, 2, 4, 5).reshape(tile_rows, tile_cols, FRAMES * 16, features)


def from_tiles(tiles):
    tile_rows = tiles.shape[0]
    tile_cols = tiles.shape[1]
    features = tiles.shape[-1]
    shaped = tiles.reshape(tile_rows, tile_cols, FRAMES, 4, 4, features)
    return shaped.transpose(2, 0, 3, 1, 4, 5).reshape(FRAMES * tile_rows * tile_cols * 16, features)


def window_keys(nearby, tile_rows, tile_cols):
    features = nearby.shape[-1]
    shaped = nearby.reshape(2, FRAMES, tile_rows + 2, 4, tile_cols + 2, 4, features)
    pieces = [
        shaped[:, :, row_step : row_step + tile_rows, :, col_step : col_step + tile_cols]
        for row_step in range(3)
        for col_step in range(3)
    ]
    stacked = jnp.stack(pieces, axis=1)
    ordered = stacked.transpose(0, 3, 5, 1, 2, 4, 6, 7)
    return ordered.reshape(2, tile_rows, tile_cols, 144 * FRAMES, features)


def fold_keys(window, tile_rows, tile_cols):
    features = window.shape[-1]
    portions = window.reshape(tile_rows, tile_cols, 3, 3, FRAMES, 4, 4, features)
    accumulated = jnp.zeros((FRAMES, tile_rows + 2, 4, tile_cols + 2, 4, features), jnp.float32)
    for row_step in range(3):
        for col_step in range(3):
            portion = portions[:, :, row_step, col_step].transpose(2, 0, 3, 1, 4, 5)
            accumulated = accumulated.at[
                :, row_step : row_step + tile_rows, :, col_step : col_step + tile_cols
            ].add(portion)
    return accumulated.reshape(FRAMES, 4 * (tile_rows + 2), 4 * (tile_cols + 2), features)


def key_mask(tile_rows, tile_cols, row_first, col_first, rows_all, cols_all):
    row_index = jnp.arange(tile_rows, dtype=jnp.int32)[:, None, None, None]
    col_index = jnp.arange(tile_cols, dtype=jnp.int32)[None, :, None, None]
    row_steps = jnp.arange(3, dtype=jnp.int32)[None, None, :, None]
    col_steps = jnp.arange(3, dtype=jnp.int32)[None, None, None, :]
    row_place = row_first + row_index + row_steps - 1
    col_place = col_first + col_index + col_steps - 1
    usable = (row_place >= 0) & (row_place < rows_all) & (col_place >= 0) & (col_place < cols_all)
    spread = jnp.broadcast_to(usable[..., None], (tile_rows, tile_cols, 3, 3, FRAMES * 16))
    return spread.reshape(tile_rows, tile_cols, 144 * FRAMES)


def attend(query_blocks, key_window, value_window, grad_blocks, usable):
    tile_rows, pair_count, query_count, features = query_blocks.shape
    head_count = features // HEAD_DIM
    key_count = key_window.shape[2]
    query_heads = query_blocks.reshape(tile_rows, pair_count, query_count, head_count, HEAD_DIM)
    grad_heads = grad_blocks.reshape(tile_rows, pair_count, query_count, head_count, HEAD_DIM)
    key_heads = key_window.reshape(tile_rows, pair_count, key_count, head_count, HEAD_DIM)
    value_heads = value_window.reshape(tile_rows, pair_count, key_count, head_count, HEAD_DIM)
    scaling = HEAD_DIM ** (-0.5)
    scores = (
        jnp.einsum("rcqhd,rckhd->rchqk", query_heads, key_heads, preferred_element_type=jnp.float32)
        * scaling
    )
    scores = jnp.where(usable[:, :, None, None, :], scores, masked_score)
    highest = jnp.max(scores, axis=-1, keepdims=True)
    raised = jnp.exp(scores - highest)
    weights = raised / jnp.sum(raised, axis=-1, keepdims=True)
    weights_low = weights.astype(jnp.bfloat16)
    mixed = jnp.einsum(
        "rchqk,rckhd->rcqhd", weights_low, value_heads, preferred_element_type=jnp.float32
    )
    offsets = jnp.sum(grad_heads.astype(jnp.float32) * mixed, axis=-1).transpose(0, 1, 3, 2)
    weight_grad = jnp.einsum(
        "rcqhd,rckhd->rchqk", grad_heads, value_heads, preferred_element_type=jnp.float32
    )
    score_grad = weights * (weight_grad - offsets[..., None])
    score_low = score_grad.astype(jnp.bfloat16)
    query_grad = (
        jnp.einsum("rchqk,rckhd->rcqhd", score_low, key_heads, preferred_element_type=jnp.float32)
        * scaling
    )
    key_terms = (
        jnp.einsum("rchqk,rcqhd->rckhd", score_low, query_heads, preferred_element_type=jnp.float32)
        * scaling
    )
    value_terms = jnp.einsum(
        "rchqk,rcqhd->rckhd", weights_low, grad_heads, preferred_element_type=jnp.float32
    )
    return (
        mixed.reshape(tile_rows, pair_count, query_count, features),
        query_grad.reshape(tile_rows, pair_count, query_count, features),
        key_terms.reshape(tile_rows, pair_count, key_count, features),
        value_terms.reshape(tile_rows, pair_count, key_count, features),
    )


def pass_keys(block, step):
    return from_behind(block, "tile", step)


def pass_terms(block, step):
    return from_behind(block, "tile", step)


def settle(received):
    rows_here = received.shape[-3]
    width_here = received.shape[-2]
    features = received.shape[-1]
    shaped = received.reshape(FRAMES, 4, rows_here, width_here, features).transpose(0, 2, 1, 3, 4)
    return shaped.reshape(FRAMES, 4 * rows_here, width_here, features)


def local(query_slab, key_slab, value_slab, upstream):
    query_rows, key_rows, value_rows = (
        lax.all_to_all(query_slab, "head", split_axis=3, concat_axis=2, tiled=True),
        lax.all_to_all(key_slab, "head", split_axis=3, concat_axis=2, tiled=True),
        lax.all_to_all(value_slab, "head", split_axis=3, concat_axis=2, tiled=True),
    )
    owner_count = lax.axis_size("tile")
    row_groups = owner_count // 4
    source_count = query_rows.shape[0]
    features = query_rows.shape[3]
    tile_rows = query_rows.shape[1] // row_groups
    tile_cols = FRAME_W // 16
    band_width = 4 * tile_cols
    line_count = 4 * tile_rows
    owner_index = lax.axis_index("tile")
    row_group = owner_index // 4
    col_group = owner_index % 4
    left_ok = col_group > 0
    right_ok = col_group < 3

    def to_owners(slab):
        shaped = slab.reshape(source_count, row_groups, tile_rows, 4, band_width, features)
        return shaped.transpose(1, 3, 0, 2, 4, 5).reshape(
            owner_count, source_count, tile_rows, band_width, features
        )

    query_got, key_got, value_got = (
        lax.all_to_all(to_owners(query_rows), "tile", split_axis=0, concat_axis=1, tiled=True),
        lax.all_to_all(to_owners(key_rows), "tile", split_axis=0, concat_axis=1, tiled=True),
        lax.all_to_all(to_owners(value_rows), "tile", split_axis=0, concat_axis=1, tiled=True),
    )
    owned_query = settle(query_got)
    owned_pair = jnp.stack((settle(key_got), settle(value_got)))
    from_left = pass_keys(owned_pair[:, :, :, band_width - 4 :], 1)
    from_right = pass_keys(owned_pair[:, :, :, 0:4], -1)
    from_left = jnp.where(left_ok, from_left, jnp.zeros_like(from_left))
    from_right = jnp.where(right_ok, from_right, jnp.zeros_like(from_right))
    wide_pair = jnp.concatenate((from_left, owned_pair, from_right), axis=3)
    from_above = pass_keys(wide_pair, 4)
    from_below = pass_keys(wide_pair, -4)
    nearby = jnp.concatenate((from_above, wide_pair, from_below), axis=2)
    query_tiles = to_tiles(owned_query, tile_rows, tile_cols)
    grad_tiles = to_tiles(
        upstream.reshape(FRAMES, line_count, band_width, features), tile_rows, tile_cols
    )
    usable = key_mask(
        tile_rows,
        tile_cols,
        row_group * tile_rows,
        col_group * tile_cols,
        row_groups * tile_rows,
        4 * tile_cols,
    )
    totals = jnp.zeros((2, FRAMES, line_count + 8, band_width + 8, features), jnp.float32)

    def one_column(totals, column):
        first_col = column * 4
        nearby_part = lax.dynamic_slice_in_dim(nearby, first_col, 12, 3)
        windows = window_keys(nearby_part, tile_rows, 1)
        query_part = lax.dynamic_slice_in_dim(query_tiles, column, 1, 1)
        grad_part = lax.dynamic_slice_in_dim(grad_tiles, column, 1, 1)
        usable_part = lax.dynamic_slice_in_dim(usable, column, 1, 1)
        mixed, query_grad, key_terms, value_terms = attend(
            query_part, windows[0], windows[1], grad_part, usable_part
        )
        folded = jnp.stack(
            (fold_keys(key_terms, tile_rows, 1), fold_keys(value_terms, tile_rows, 1))
        )
        current = lax.dynamic_slice_in_dim(totals, first_col, 12, 3)
        totals = lax.dynamic_update_slice_in_dim(totals, current + folded, first_col, 3)
        return (totals, (mixed[:, 0].astype(jnp.bfloat16), query_grad[:, 0].astype(jnp.bfloat16)))

    extended, (mixed, query_grad) = lax.scan(
        one_column, totals, jnp.arange(tile_cols, dtype=jnp.int32)
    )
    attended = from_tiles(jnp.swapaxes(mixed, 0, 1))
    query_out = from_tiles(jnp.swapaxes(query_grad, 0, 1))
    top_band = extended[:, :, 0:4].astype(jnp.bfloat16)
    bottom_band = extended[:, :, line_count + 4 :].astype(jnp.bfloat16)
    terms_below = pass_terms(top_band, -4).astype(jnp.float32)
    terms_above = pass_terms(bottom_band, 4).astype(jnp.float32)
    incoming = terms_above
    incoming = incoming + terms_below
    rowed = extended[:, :, 4 : line_count + 4] + incoming
    left_terms = rowed[:, :, :, 0:4].astype(jnp.bfloat16)
    right_terms = rowed[:, :, :, band_width + 4 :].astype(jnp.bfloat16)
    terms_right = pass_terms(left_terms, -1)
    terms_left = pass_terms(right_terms, 1)
    terms_right = jnp.where(right_ok, terms_right, jnp.zeros_like(terms_right)).astype(jnp.float32)
    terms_left = jnp.where(left_ok, terms_left, jnp.zeros_like(terms_left)).astype(jnp.float32)
    summed = rowed[:, :, :, 4 : band_width + 4]
    summed = summed + jnp.pad(terms_left, ((0, 0), (0, 0), (0, 0), (0, band_width - 4), (0, 0)))
    summed = summed + jnp.pad(terms_right, ((0, 0), (0, 0), (0, 0), (band_width - 4, 0), (0, 0)))
    summed = summed.astype(jnp.bfloat16)
    key_grad = summed[0].reshape(-1, features)
    value_grad = summed[1].reshape(-1, features)
    return (attended, query_out, key_grad, value_grad)


SLOTS = 14


def fast_kernel(send_ref, up_ref, attended_ref, query_ref, key_ref, value_ref, qkv, gbuf, obuf, acc, landed, rims,
                main_send, main_recv, ext_send, ext_recv, left_send, left_recv, right_send, right_recv,
                up_send, up_recv, upx_send, upx_recv, out_send, out_recv, outx_send, outx_recv,
                rim_send, rim_recv):
    tile = lax.axis_index("tile")
    head = lax.axis_index("head")
    me = tile * 4 + head
    row_half = tile // 4
    col = tile % 4

    barrier = pltpu.get_barrier_semaphore()

    def greet(step, carry):
        other = (me + step) % 32
        pl.semaphore_signal(barrier, inc=1, device_id=(other // 4, other % 4), device_id_type=MESH)
        return carry

    lax.fori_loop(1, 32, greet, 0)
    pl.semaphore_wait(barrier, 31)

    def push(src, dst, send_sem, recv_sem, to_tile, to_head):
        return pltpu.make_async_remote_copy(
            src_ref=src, dst_ref=dst, send_sem=send_sem, recv_sem=recv_sem,
            device_id=(to_tile, to_head), device_id_type=MESH)

    def landing(dst, recv_sem):
        return pltpu.make_async_copy(dst, dst, recv_sem)

    rows = pl.ds(16 * row_half, 16)

    def ext_parts(which):
        to_head, extra = which // 2, which % 2
        return to_head, extra, to_head * 10 + 8 + extra

    def ext_copy(which):
        to_head, extra, source = ext_parts(which)
        return push(send_ref.at[source], qkv.at[:, pl.ds(11, 2), tile],
                    ext_send.at[which], ext_recv.at[tile], 4 * extra + head, to_head)

    def ext_is_own(which):
        to_head, extra, source = ext_parts(which)
        return (4 * extra + head) * 4 + to_head == me

    def left_copy(which):
        to_head, extra, source = ext_parts(which)
        return push(send_ref.at[source, pl.ds(1, 2), 1], qkv.at[pl.ds(1, 2), 10, tile],
                    left_send.at[which], left_recv.at[tile], 4 * extra + head + 1, to_head)

    def left_is_own(which):
        to_head, extra, source = ext_parts(which)
        return (4 * extra + head + 1) * 4 + to_head == me

    def right_copy(which):
        to_head, extra, source = ext_parts(which)
        return push(send_ref.at[source, pl.ds(1, 2), 0], qkv.at[pl.ds(1, 2), 13, tile],
                    right_send.at[which], right_recv.at[tile], 4 * extra + head - 1, to_head)

    def right_is_own(which):
        to_head, extra, source = ext_parts(which)
        return (4 * extra + head - 1) * 4 + to_head == me

    def ext_start(which, carry):
        to_head, extra, source = ext_parts(which)

        @pl.when(ext_is_own(which))
        def _():
            pltpu.make_async_copy(send_ref.at[source], qkv.at[:, pl.ds(11, 2), tile], ext_recv.at[tile]).start()

        @pl.when(jnp.logical_not(ext_is_own(which)))
        def _():
            ext_copy(which).start()

        @pl.when(head < 3)
        def _():
            @pl.when(left_is_own(which))
            def _():
                pltpu.make_async_copy(send_ref.at[source, pl.ds(1, 2), 1], qkv.at[pl.ds(1, 2), 10, tile],
                                      left_recv.at[tile]).start()

            @pl.when(jnp.logical_not(left_is_own(which)))
            def _():
                left_copy(which).start()

        @pl.when(head > 0)
        def _():
            @pl.when(right_is_own(which))
            def _():
                pltpu.make_async_copy(send_ref.at[source, pl.ds(1, 2), 0], qkv.at[pl.ds(1, 2), 13, tile],
                                      right_recv.at[tile]).start()

            @pl.when(jnp.logical_not(right_is_own(which)))
            def _():
                right_copy(which).start()

        return carry

    lax.fori_loop(0, 8, ext_start, 0)

    def upx_copy(extra):
        return push(up_ref.at[8 + extra], gbuf.at[pl.ds(11, 2), :, rows],
                    upx_send.at[extra], upx_recv.at[row_half], 4 * extra + col, head)

    for extra in range(2):
        @pl.when(row_half == extra)
        def _(extra=extra):
            pltpu.make_async_copy(up_ref.at[8 + extra], gbuf.at[pl.ds(11, 2), :, rows],
                                  upx_recv.at[row_half]).start()

        @pl.when(row_half != extra)
        def _(extra=extra):
            upx_copy(extra).start()

    def up_copy(other):
        return push(up_ref.at[other], gbuf.at[pl.ds(1 + 2 * col, 2), :, rows],
                    up_send.at[other], up_recv.at[tile], other, head)

    def up_start(step, carry):
        up_copy((tile + 3 + step + step // 5) % 8).start()
        return carry

    lax.fori_loop(1, 8, up_start, 0)
    pltpu.make_async_copy(up_ref.at[tile], gbuf.at[pl.ds(1 + 2 * col, 2), :, rows], up_recv.at[tile]).start()

    def main_copy(other):
        to_tile, to_head = other // 4, other % 4
        src = send_ref.at[to_head * 10 + to_tile]
        dst = qkv.at[:, pl.ds(1 + 2 * head, 2), tile]
        return push(src, dst, main_send.at[other], main_recv.at[me], to_tile, to_head)

    def main_peer(place):
        turn = place // 4
        shift = 12 + ((turn + 1) // 2) * (2 * (turn % 2) - 1)
        return ((tile + shift) % 8) * 4 + (head + place) % 4

    def main_start(place, carry):
        main_copy(main_peer(place)).start()
        return carry

    lax.fori_loop(0, 28, main_start, 0)
    lax.fori_loop(29, 32, main_start, 0)
    pltpu.make_async_copy(send_ref.at[head * 10 + tile], qkv.at[:, pl.ds(1 + 2 * head, 2), tile],
                          main_recv.at[me]).start()

    blank = jnp.zeros((FRAMES, 32, HEAD_DIM), jnp.bfloat16)
    for part in (1, 2):
        qkv[part, 0] = blank
        qkv[part, 9] = blank

        @pl.when(col == 0)
        def _(part=part):
            qkv[part, 10] = blank

        @pl.when(col == 3)
        def _(part=part):
            qkv[part, 13] = blank

    acc[...] = jnp.zeros_like(acc)

    scaling = HEAD_DIM ** (-0.5)
    key_at = lax.broadcasted_iota(jnp.int32, (768, 1), 0)

    def one_tile(job):
        first = job + 2 * (job // 8)
        low = jnp.where((job == 0) | ((job == 8) & (col == 0)), 256, 0)
        high = jnp.where((job == 7) | ((job == 9) & (col == 3)), 512, 768)
        usable = (key_at >= low) & (key_at < high)
        bias = jnp.where(usable, 0.0, -1e30)
        query = qkv[0, first + 1].reshape(256, HEAD_DIM)
        grad = gbuf[first + 1].reshape(256, HEAD_DIM)
        keys = qkv[1, pl.ds(first, 3)].reshape(768, HEAD_DIM)
        values = qkv[2, pl.ds(first, 3)].reshape(768, HEAD_DIM)
        scores = lax.dot_general(keys, query, (((1,), (1,)), ((), ())), preferred_element_type=jnp.float32)
        scores = scores * (scaling * math.log2(math.e)) + bias
        highest = jnp.max(scores, axis=0, keepdims=True)
        raised = jnp.exp2(scores - highest)
        weights = raised * (1.0 / jnp.sum(raised, axis=0, keepdims=True))
        weights_low = weights.astype(jnp.bfloat16)
        mixed = lax.dot_general(values, weights_low, (((0,), (0,)), ((), ())), preferred_element_type=jnp.float32)
        grad_across = grad.astype(jnp.float32).T
        offsets = jnp.sum(grad_across * mixed, axis=0, keepdims=True)
        weight_grad = lax.dot_general(values, grad, (((1,), (1,)), ((), ())), preferred_element_type=jnp.float32)
        score_low = (weights * (weight_grad - offsets)).astype(jnp.bfloat16)
        query_grad = lax.dot_general(keys, score_low, (((0,), (0,)), ((), ())), preferred_element_type=jnp.float32)
        obuf[0, first + 1] = mixed.T.astype(jnp.bfloat16).reshape(FRAMES, 32, HEAD_DIM)
        obuf[1, first + 1] = (query_grad * scaling).T.astype(jnp.bfloat16).reshape(FRAMES, 32, HEAD_DIM)
        key_terms = lax.dot_general(score_low, query, (((1,), (0,)), ((), ())), preferred_element_type=jnp.float32)
        value_terms = lax.dot_general(weights_low, grad, (((1,), (0,)), ((), ())), preferred_element_type=jnp.float32)
        acc[0, pl.ds(first, 3)] += (key_terms * scaling).reshape(3, 256, HEAD_DIM)
        acc[1, pl.ds(first, 3)] += value_terms.reshape(3, 256, HEAD_DIM)

    def settle(slot):
        for part in range(2):
            obuf[2 + part, slot] = acc[part, slot].astype(jnp.bfloat16).reshape(FRAMES, 32, HEAD_DIM)

    def out_piece(pair, other):
        return obuf.at[pl.ds(2 * pair, 2), pl.ds(1 + 2 * (other % 4), 2), :, pl.ds(16 * (other // 4), 16)]

    def out_copy(pair, other):
        return push(out_piece(pair, other), landed.at[pl.ds(2 * pair, 2), tile],
                    out_send.at[pair, other], out_recv.at[pair, tile], other, head)

    def out_start(pair, column):
        for step in (1, 0):
            other = 4 * ((row_half + step) % 2) + column

            @pl.when(other == tile)
            def _(other=other):
                pltpu.make_async_copy(out_piece(pair, other), landed.at[pl.ds(2 * pair, 2), tile],
                                      out_recv.at[pair, tile]).start()

            @pl.when(other != tile)
            def _(other=other):
                out_copy(pair, other).start()

    def outx_copy(half):
        return push(obuf.at[:, pl.ds(11, 2), :, pl.ds(16 * half, 16)], landed.at[:, 8 + row_half],
                    outx_send.at[half], outx_recv.at[row_half], 4 * half + col, head)

    def rim_copy(half, side):
        slot, step = ((13, 1), (10, -1))[side]
        return push(obuf.at[pl.ds(2, 2), slot, :, pl.ds(16 * half, 16)], rims.at[row_half, side],
                    rim_send.at[half, side], rim_recv.at[row_half, side], 4 * half + col + step, head)

    def ext_arrive(frame, carry):
        landing(qkv.at[:, pl.ds(11, 2), frame], ext_recv.at[frame]).wait()

        @pl.when(col > 0)
        def _():
            landing(qkv.at[pl.ds(1, 2), 10, frame], left_recv.at[frame]).wait()

        @pl.when(col < 3)
        def _():
            landing(qkv.at[pl.ds(1, 2), 13, frame], right_recv.at[frame]).wait()

        return carry

    lax.fori_loop(0, 8, ext_arrive, 0)

    for half in range(2):
        landing(gbuf.at[pl.ds(11, 2), :, pl.ds(16 * half, 16)], upx_recv.at[half]).wait()

    def ext_tile(job, carry):
        one_tile(job)
        return carry

    lax.fori_loop(8, 10, ext_tile, 0)
    for slot in range(10, SLOTS):
        settle(slot)
    for half in range(2):
        @pl.when(row_half == half)
        def _(half=half):
            pltpu.make_async_copy(obuf.at[:, pl.ds(11, 2), :, pl.ds(16 * half, 16)], landed.at[:, 8 + row_half],
                                  outx_recv.at[row_half]).start()

        @pl.when(row_half != half)
        def _(half=half):
            outx_copy(half).start()

        @pl.when(col < 3)
        def _(half=half):
            rim_copy(half, 0).start()

        @pl.when(col > 0)
        def _(half=half):
            rim_copy(half, 1).start()

    for extra in range(2):
        @pl.when(col == 0)
        def _(extra=extra):
            rims[extra, 0] = jnp.zeros((2, FRAMES, 16, HEAD_DIM), jnp.bfloat16)

        @pl.when(col == 3)
        def _(extra=extra):
            rims[extra, 1] = jnp.zeros((2, FRAMES, 16, HEAD_DIM), jnp.bfloat16)

    def main_arrive(other, carry):
        landing(qkv.at[:, pl.ds(1 + 2 * (other % 4), 2), other // 4], main_recv.at[other]).wait()
        return carry

    lax.fori_loop(0, 32, main_arrive, 0)

    def up_arrive(other, carry):
        landing(gbuf.at[pl.ds(1 + 2 * (other % 4), 2), :, pl.ds(16 * (other // 4), 16)], up_recv.at[other]).wait()
        return carry

    lax.fori_loop(0, 8, up_arrive, 0)
    def settle_column(column):
        settle(1 + 2 * column)
        settle(2 + 2 * column)
        out_start(1, column)

    def main_tile(step, carry):
        one_tile((step + 2 * col) % 8)

        @pl.when(step % 2 == 1)
        def _():
            out_start(0, (col + step // 2) % 4)

        @pl.when((step == 4) | (step == 6))
        def _():
            settle_column((col + step // 2 - 1) % 4)

        return carry

    lax.fori_loop(0, 8, main_tile, 0)
    settle_column((col + 3) % 4)
    settle_column(col)

    upper = lax.broadcasted_iota(jnp.int32, (16, 8, HEAD_DIM), 1) < 4

    def place(ref, which, near, far):
        near = near.reshape(16, 8, HEAD_DIM)
        far = far.reshape(16, 8, HEAD_DIM)
        even = jnp.where(upper, near, pltpu.roll(far, 4, 1))
        odd = jnp.where(upper, pltpu.roll(near, 4, 1), far)
        lines = jnp.stack((even, odd), axis=1).reshape(256, HEAD_DIM)
        ref[:, pl.ds(pl.multiple_of(which * HEAD_DIM, HEAD_DIM), HEAD_DIM)] = lines.astype(jnp.bfloat16)

    out_refs = (attended_ref, query_ref, key_ref, value_ref)

    def wide(part, which, side):
        return landed[part, which, side].astype(jnp.float32)

    for extra in range(2):
        landing(landed.at[:, 8 + extra], outx_recv.at[extra]).wait()

        @pl.when(col > 0)
        def _(extra=extra):
            landing(rims.at[extra, 0], rim_recv.at[extra, 0]).wait()

        @pl.when(col < 3)
        def _(extra=extra):
            landing(rims.at[extra, 1], rim_recv.at[extra, 1]).wait()

        for part in range(2):
            place(out_refs[part], 8 + extra, wide(part, 8 + extra, 0), wide(part, 8 + extra, 1))
            place(out_refs[2 + part], 8 + extra,
                  wide(2 + part, 8 + extra, 0) + rims[extra, 0, part].astype(jnp.float32),
                  wide(2 + part, 8 + extra, 1) + rims[extra, 1, part].astype(jnp.float32))

    for pair in range(2):
        def out_arrive(step, carry, pair=pair):
            other = (tile + step) % 8
            landing(landed.at[pl.ds(2 * pair, 2), other], out_recv.at[pair, other]).wait()
            for part in (2 * pair, 2 * pair + 1):
                place(out_refs[part], other, wide(part, other, 0), wide(part, other, 1))
            return carry

        lax.fori_loop(0, 8, out_arrive, 0)

    def main_left(step, carry):
        main_copy((me + step) % 32).wait_send()
        return carry

    lax.fori_loop(1, 32, main_left, 0)

    def group_left(step, carry):
        up_copy((tile + step) % 8).wait_send()
        out_copy(0, (tile + step) % 8).wait_send()
        out_copy(1, (tile + step) % 8).wait_send()
        return carry

    lax.fori_loop(1, 8, group_left, 0)

    def ext_left(which, carry):
        @pl.when(jnp.logical_not(ext_is_own(which)))
        def _():
            ext_copy(which).wait_send()

        @pl.when((head < 3) & jnp.logical_not(left_is_own(which)))
        def _():
            left_copy(which).wait_send()

        @pl.when((head > 0) & jnp.logical_not(right_is_own(which)))
        def _():
            right_copy(which).wait_send()

        return carry

    lax.fori_loop(0, 8, ext_left, 0)
    for half in range(2):
        @pl.when(row_half != half)
        def _(half=half):
            upx_copy(half).wait_send()
            outx_copy(half).wait_send()

        @pl.when(col < 3)
        def _(half=half):
            rim_copy(half, 0).wait_send()

        @pl.when(col > 0)
        def _(half=half):
            rim_copy(half, 1).wait_send()


def fast_local(query_slab, key_slab, value_slab, upstream):
    def by_head(slab):
        shaped = slab.reshape(4, 2, 2, 4, 40, HEAD_DIM).transpose(4, 2, 1, 0, 3, 5)
        return shaped.reshape(40, 2, 32, HEAD_DIM)

    send = jnp.stack((by_head(query_slab), by_head(key_slab), by_head(value_slab)), axis=1)
    up = upstream.reshape(FRAMES, 4, 2, 4, 10, HEAD_DIM).transpose(4, 2, 0, 1, 3, 5)
    up = up.reshape(10, 2, FRAMES, 16, HEAD_DIM)
    dma = pltpu.SemaphoreType.DMA
    out = pl.pallas_call(
        fast_kernel,
        out_shape=[jax.ShapeDtypeStruct((256, 10 * HEAD_DIM), jnp.bfloat16)] * 4,
        in_specs=[pl.BlockSpec(memory_space=pltpu.VMEM)] * 2,
        out_specs=[pl.BlockSpec(memory_space=pltpu.VMEM)] * 4,
        scratch_shapes=[
            pltpu.VMEM((3, SLOTS, FRAMES, 32, HEAD_DIM), jnp.bfloat16),
            pltpu.VMEM((SLOTS, FRAMES, 32, HEAD_DIM), jnp.bfloat16),
            pltpu.VMEM((4, SLOTS, FRAMES, 32, HEAD_DIM), jnp.bfloat16),
            pltpu.VMEM((2, SLOTS, 256, HEAD_DIM), jnp.float32),
            pltpu.VMEM((4, 10, 2, FRAMES, 16, HEAD_DIM), jnp.bfloat16),
            pltpu.VMEM((2, 2, 2, FRAMES, 16, HEAD_DIM), jnp.bfloat16),
            dma((32,)), dma((32,)), dma((8,)), dma((8,)), dma((8,)), dma((8,)), dma((8,)), dma((8,)),
            dma((8,)), dma((8,)), dma((2,)), dma((2,)), dma((2, 8)), dma((2, 8)), dma((2,)), dma((2,)),
            dma((2, 2)), dma((2, 2)),
        ],
        compiler_params=pltpu.CompilerParams(
            collective_id=0, has_side_effects=True, vmem_limit_bytes=48 * 1024 * 1024
        ),
        cost_estimate=pl.CostEstimate(flops=3 * 10**9, bytes_accessed=8 * 10**6, transcendentals=2 * 10**6),
    )(send, up)
    return tuple(out)


def solution(mesh):
    placed = (
        P("tile", None, "head", None),
        P("tile", None, "head", None),
        P("tile", None, "head", None),
        P("tile", "head"),
    )

    def chosen(query_slab, key_slab, value_slab, upstream):
        two_rows = query_slab.shape == (4, 2, 8, 40 * HEAD_DIM) and upstream.shape == (256, 10 * HEAD_DIM)
        body = fast_local if two_rows and mesh.shape["tile"] == 8 and mesh.shape["head"] == 4 else local
        return body(query_slab, key_slab, value_slab, upstream)

    return jax.shard_map(
        chosen,
        mesh=mesh,
        in_specs=placed,
        out_specs=(P("tile", "head"), P("tile", "head"), P("tile", "head"), P("tile", "head")),
        check_vma=False,
    )
```

```python
import math

import jax
import jax.numpy as jnp
from jax import lax
from jax.experimental import pallas as pl
from jax.experimental.pallas import tpu as pltpu
from jax.sharding import PartitionSpec as P

HEAD_DIM = 128
FRAMES = 8
FRAME_W = 32
MESH = pl.DeviceIdType.MESH


masked_score = -1e30


def from_behind(value, axis, steps):
    count = lax.axis_size(axis)
    leading, last = (max(0, -steps), min(count, count - steps))
    return lax.ppermute(value, axis, [(source, source + steps) for source in range(leading, last)])


def to_tiles(grid, tile_rows, tile_cols):
    features = grid.shape[-1]
    shaped = grid.reshape(FRAMES, tile_rows, 4, tile_cols, 4, features)
    return shaped.transpose(1, 3, 0, 2, 4, 5).reshape(tile_rows, tile_cols, FRAMES * 16, features)


def from_tiles(tiles):
    tile_rows = tiles.shape[0]
    tile_cols = tiles.shape[1]
    features = tiles.shape[-1]
    shaped = tiles.reshape(tile_rows, tile_cols, FRAMES, 4, 4, features)
    return shaped.transpose(2, 0, 3, 1, 4, 5).reshape(FRAMES * tile_rows * tile_cols * 16, features)


def window_keys(nearby, tile_rows, tile_cols):
    features = nearby.shape[-1]
    shaped = nearby.reshape(2, FRAMES, tile_rows + 2, 4, tile_cols + 2, 4, features)
    pieces = [
        shaped[:, :, row_step : row_step + tile_rows, :, col_step : col_step + tile_cols]
        for row_step in range(3)
        for col_step in range(3)
    ]
    stacked = jnp.stack(pieces, axis=1)
    ordered = stacked.transpose(0, 3, 5, 1, 2, 4, 6, 7)
    return ordered.reshape(2, tile_rows, tile_cols, 144 * FRAMES, features)


def fold_keys(window, tile_rows, tile_cols):
    features = window.shape[-1]
    portions = window.reshape(tile_rows, tile_cols, 3, 3, FRAMES, 4, 4, features)
    accumulated = jnp.zeros((FRAMES, tile_rows + 2, 4, tile_cols + 2, 4, features), jnp.float32)
    for row_step in range(3):
        for col_step in range(3):
            portion = portions[:, :, row_step, col_step].transpose(2, 0, 3, 1, 4, 5)
            accumulated = accumulated.at[
                :, row_step : row_step + tile_rows, :, col_step : col_step + tile_cols
            ].add(portion)
    return accumulated.reshape(FRAMES, 4 * (tile_rows + 2), 4 * (tile_cols + 2), features)


def key_mask(tile_rows, tile_cols, row_first, col_first, rows_all, cols_all):
    row_index = jnp.arange(tile_rows, dtype=jnp.int32)[:, None, None, None]
    col_index = jnp.arange(tile_cols, dtype=jnp.int32)[None, :, None, None]
    row_steps = jnp.arange(3, dtype=jnp.int32)[None, None, :, None]
    col_steps = jnp.arange(3, dtype=jnp.int32)[None, None, None, :]
    row_place = row_first + row_index + row_steps - 1
    col_place = col_first + col_index + col_steps - 1
    usable = (row_place >= 0) & (row_place < rows_all) & (col_place >= 0) & (col_place < cols_all)
    spread = jnp.broadcast_to(usable[..., None], (tile_rows, tile_cols, 3, 3, FRAMES * 16))
    return spread.reshape(tile_rows, tile_cols, 144 * FRAMES)


def attend(query_blocks, key_window, value_window, grad_blocks, usable):
    tile_rows, pair_count, query_count, features = query_blocks.shape
    head_count = features // HEAD_DIM
    key_count = key_window.shape[2]
    query_heads = query_blocks.reshape(tile_rows, pair_count, query_count, head_count, HEAD_DIM)
    grad_heads = grad_blocks.reshape(tile_rows, pair_count, query_count, head_count, HEAD_DIM)
    key_heads = key_window.reshape(tile_rows, pair_count, key_count, head_count, HEAD_DIM)
    value_heads = value_window.reshape(tile_rows, pair_count, key_count, head_count, HEAD_DIM)
    scaling = HEAD_DIM ** (-0.5)
    scores = (
        jnp.einsum("rcqhd,rckhd->rchqk", query_heads, key_heads, preferred_element_type=jnp.float32)
        * scaling
    )
    scores = jnp.where(usable[:, :, None, None, :], scores, masked_score)
    highest = jnp.max(scores, axis=-1, keepdims=True)
    raised = jnp.exp(scores - highest)
    weights = raised / jnp.sum(raised, axis=-1, keepdims=True)
    weights_low = weights.astype(jnp.bfloat16)
    mixed = jnp.einsum(
        "rchqk,rckhd->rcqhd", weights_low, value_heads, preferred_element_type=jnp.float32
    )
    offsets = jnp.sum(grad_heads.astype(jnp.float32) * mixed, axis=-1).transpose(0, 1, 3, 2)
    weight_grad = jnp.einsum(
        "rcqhd,rckhd->rchqk", grad_heads, value_heads, preferred_element_type=jnp.float32
    )
    score_grad = weights * (weight_grad - offsets[..., None])
    score_low = score_grad.astype(jnp.bfloat16)
    query_grad = (
        jnp.einsum("rchqk,rckhd->rcqhd", score_low, key_heads, preferred_element_type=jnp.float32)
        * scaling
    )
    key_terms = (
        jnp.einsum("rchqk,rcqhd->rckhd", score_low, query_heads, preferred_element_type=jnp.float32)
        * scaling
    )
    value_terms = jnp.einsum(
        "rchqk,rcqhd->rckhd", weights_low, grad_heads, preferred_element_type=jnp.float32
    )
    return (
        mixed.reshape(tile_rows, pair_count, query_count, features),
        query_grad.reshape(tile_rows, pair_count, query_count, features),
        key_terms.reshape(tile_rows, pair_count, key_count, features),
        value_terms.reshape(tile_rows, pair_count, key_count, features),
    )


def pass_keys(block, step):
    return from_behind(block, "tile", step)


def pass_terms(block, step):
    return from_behind(block, "tile", step)


def settle(received):
    rows_here = received.shape[-3]
    width_here = received.shape[-2]
    features = received.shape[-1]
    shaped = received.reshape(FRAMES, 4, rows_here, width_here, features).transpose(0, 2, 1, 3, 4)
    return shaped.reshape(FRAMES, 4 * rows_here, width_here, features)


def local(query_slab, key_slab, value_slab, upstream):
    query_rows, key_rows, value_rows = (
        lax.all_to_all(query_slab, "head", split_axis=3, concat_axis=2, tiled=True),
        lax.all_to_all(key_slab, "head", split_axis=3, concat_axis=2, tiled=True),
        lax.all_to_all(value_slab, "head", split_axis=3, concat_axis=2, tiled=True),
    )
    owner_count = lax.axis_size("tile")
    row_groups = owner_count // 4
    source_count = query_rows.shape[0]
    features = query_rows.shape[3]
    tile_rows = query_rows.shape[1] // row_groups
    tile_cols = FRAME_W // 16
    band_width = 4 * tile_cols
    line_count = 4 * tile_rows
    owner_index = lax.axis_index("tile")
    row_group = owner_index // 4
    col_group = owner_index % 4
    left_ok = col_group > 0
    right_ok = col_group < 3

    def to_owners(slab):
        shaped = slab.reshape(source_count, row_groups, tile_rows, 4, band_width, features)
        return shaped.transpose(1, 3, 0, 2, 4, 5).reshape(
            owner_count, source_count, tile_rows, band_width, features
        )

    query_got, key_got, value_got = (
        lax.all_to_all(to_owners(query_rows), "tile", split_axis=0, concat_axis=1, tiled=True),
        lax.all_to_all(to_owners(key_rows), "tile", split_axis=0, concat_axis=1, tiled=True),
        lax.all_to_all(to_owners(value_rows), "tile", split_axis=0, concat_axis=1, tiled=True),
    )
    owned_query = settle(query_got)
    owned_pair = jnp.stack((settle(key_got), settle(value_got)))
    from_left = pass_keys(owned_pair[:, :, :, band_width - 4 :], 1)
    from_right = pass_keys(owned_pair[:, :, :, 0:4], -1)
    from_left = jnp.where(left_ok, from_left, jnp.zeros_like(from_left))
    from_right = jnp.where(right_ok, from_right, jnp.zeros_like(from_right))
    wide_pair = jnp.concatenate((from_left, owned_pair, from_right), axis=3)
    from_above = pass_keys(wide_pair, 4)
    from_below = pass_keys(wide_pair, -4)
    nearby = jnp.concatenate((from_above, wide_pair, from_below), axis=2)
    query_tiles = to_tiles(owned_query, tile_rows, tile_cols)
    grad_tiles = to_tiles(
        upstream.reshape(FRAMES, line_count, band_width, features), tile_rows, tile_cols
    )
    usable = key_mask(
        tile_rows,
        tile_cols,
        row_group * tile_rows,
        col_group * tile_cols,
        row_groups * tile_rows,
        4 * tile_cols,
    )
    totals = jnp.zeros((2, FRAMES, line_count + 8, band_width + 8, features), jnp.float32)

    def one_column(totals, column):
        first_col = column * 4
        nearby_part = lax.dynamic_slice_in_dim(nearby, first_col, 12, 3)
        windows = window_keys(nearby_part, tile_rows, 1)
        query_part = lax.dynamic_slice_in_dim(query_tiles, column, 1, 1)
        grad_part = lax.dynamic_slice_in_dim(grad_tiles, column, 1, 1)
        usable_part = lax.dynamic_slice_in_dim(usable, column, 1, 1)
        mixed, query_grad, key_terms, value_terms = attend(
            query_part, windows[0], windows[1], grad_part, usable_part
        )
        folded = jnp.stack(
            (fold_keys(key_terms, tile_rows, 1), fold_keys(value_terms, tile_rows, 1))
        )
        current = lax.dynamic_slice_in_dim(totals, first_col, 12, 3)
        totals = lax.dynamic_update_slice_in_dim(totals, current + folded, first_col, 3)
        return (totals, (mixed[:, 0].astype(jnp.bfloat16), query_grad[:, 0].astype(jnp.bfloat16)))

    extended, (mixed, query_grad) = lax.scan(
        one_column, totals, jnp.arange(tile_cols, dtype=jnp.int32)
    )
    attended = from_tiles(jnp.swapaxes(mixed, 0, 1))
    query_out = from_tiles(jnp.swapaxes(query_grad, 0, 1))
    top_band = extended[:, :, 0:4].astype(jnp.bfloat16)
    bottom_band = extended[:, :, line_count + 4 :].astype(jnp.bfloat16)
    terms_below = pass_terms(top_band, -4).astype(jnp.float32)
    terms_above = pass_terms(bottom_band, 4).astype(jnp.float32)
    incoming = terms_above
    incoming = incoming + terms_below
    rowed = extended[:, :, 4 : line_count + 4] + incoming
    left_terms = rowed[:, :, :, 0:4].astype(jnp.bfloat16)
    right_terms = rowed[:, :, :, band_width + 4 :].astype(jnp.bfloat16)
    terms_right = pass_terms(left_terms, -1)
    terms_left = pass_terms(right_terms, 1)
    terms_right = jnp.where(right_ok, terms_right, jnp.zeros_like(terms_right)).astype(jnp.float32)
    terms_left = jnp.where(left_ok, terms_left, jnp.zeros_like(terms_left)).astype(jnp.float32)
    summed = rowed[:, :, :, 4 : band_width + 4]
    summed = summed + jnp.pad(terms_left, ((0, 0), (0, 0), (0, 0), (0, band_width - 4), (0, 0)))
    summed = summed + jnp.pad(terms_right, ((0, 0), (0, 0), (0, 0), (band_width - 4, 0), (0, 0)))
    summed = summed.astype(jnp.bfloat16)
    key_grad = summed[0].reshape(-1, features)
    value_grad = summed[1].reshape(-1, features)
    return (attended, query_out, key_grad, value_grad)


SLOTS = 14


def fast_kernel(query_slab, key_slab, value_slab, grad_in, attended_ref, query_ref, key_ref, value_ref,
                send_ref, up_ref, qkv, gbuf, obuf, acc, landed, rims,
                main_send, main_recv, ext_send, ext_recv, side_send, side_recv,
                up_send, up_recv, upx_send, upx_recv, out_send, out_recv, outx_send, outx_recv,
                rim_send, rim_recv):
    tile = lax.axis_index("tile")
    head = lax.axis_index("head")
    me = tile * 4 + head
    row_half = tile // 4
    col = tile % 4

    barrier = pltpu.get_barrier_semaphore()

    def greet(step, carry):
        other = (me + step) % 32
        pl.semaphore_signal(barrier, inc=1, device_id=(other // 4, other % 4), device_id_type=MESH)
        return carry

    lax.fori_loop(1, 32, greet, 0)

    def regroup(first, second):
        upper = lax.broadcasted_iota(jnp.int32, first.shape, first.ndim - 2) < 4
        near = jnp.where(upper, first, pltpu.roll(second, 4, first.ndim - 2))
        far = jnp.where(upper, pltpu.roll(first, 4, first.ndim - 2), second)
        return near, far

    def lanes(which):
        return pl.ds(pl.multiple_of(which * HEAD_DIM, HEAD_DIM), HEAD_DIM)

    def prepare(which):
        for part, slab in enumerate((query_slab, key_slab, value_slab)):
            lines = slab[:, :, :, lanes(which)].astype(jnp.float32).reshape(2, 2, 16, HEAD_DIM)
            first = lines[:, 0].reshape(4, 8, HEAD_DIM)
            second = lines[:, 1].reshape(4, 8, HEAD_DIM)
            for side, taken in enumerate(regroup(first, second)):
                ordered = jnp.stack((taken[0], taken[2], taken[1], taken[3])).reshape(32, HEAD_DIM)
                send_ref[which, part, side] = ordered.astype(jnp.bfloat16)

    def prepare_up(which):
        lines = grad_in[:, lanes(which)].astype(jnp.float32).reshape(16, 2, 8, HEAD_DIM)
        for side, taken in enumerate(regroup(lines[:, 0], lines[:, 1])):
            up_ref[which, side] = taken.reshape(FRAMES, 16, HEAD_DIM).astype(jnp.bfloat16)

    def prepare_shared(which, carry):
        prepare((which // 2) * 10 + 8 + which % 2)
        return carry

    lax.fori_loop(0, 8, prepare_shared, 0)
    pl.semaphore_wait(barrier, 31)

    def push(src, dst, send_sem, recv_sem, to_tile, to_head):
        return pltpu.make_async_remote_copy(
            src_ref=src, dst_ref=dst, send_sem=send_sem, recv_sem=recv_sem,
            device_id=(to_tile, to_head), device_id_type=MESH)

    def landing(dst, recv_sem):
        return pltpu.make_async_copy(dst, dst, recv_sem)

    rows = pl.ds(16 * row_half, 16)

    def ext_parts(which):
        to_head, extra = which // 2, which % 2
        return to_head, extra, to_head * 10 + 8 + extra

    def ext_copy(which):
        to_head, extra, source = ext_parts(which)
        return push(send_ref.at[source], qkv.at[:, pl.ds(11, 2), tile],
                    ext_send.at[which], ext_recv.at[tile], 4 * extra + head, to_head)

    def ext_is_own(which):
        to_head, extra, source = ext_parts(which)
        return (4 * extra + head) * 4 + to_head == me

    def ext_start(which, carry):
        to_head, extra, source = ext_parts(which)

        @pl.when(ext_is_own(which))
        def _():
            pltpu.make_async_copy(send_ref.at[source], qkv.at[:, pl.ds(11, 2), tile], ext_recv.at[tile]).start()

        @pl.when(jnp.logical_not(ext_is_own(which)))
        def _():
            ext_copy(which).start()

        return carry

    lax.fori_loop(0, 8, ext_start, 0)

    def upx_copy(extra):
        return push(up_ref.at[8 + extra], gbuf.at[pl.ds(11, 2), :, rows],
                    upx_send.at[extra], upx_recv.at[row_half], 4 * extra + col, head)

    for extra in range(2):
        prepare_up(8 + extra)

        @pl.when(row_half == extra)
        def _(extra=extra):
            pltpu.make_async_copy(up_ref.at[8 + extra], gbuf.at[pl.ds(11, 2), :, rows],
                                  upx_recv.at[row_half]).start()

        @pl.when(row_half != extra)
        def _(extra=extra):
            upx_copy(extra).start()

    def up_copy(other):
        return push(up_ref.at[other], gbuf.at[pl.ds(1 + 2 * col, 2), :, rows],
                    up_send.at[other], up_recv.at[tile], other, head)

    def up_start(step, carry):
        other = (tile + 3 + step + step // 5) % 8
        prepare_up(other)
        up_copy(other).start()
        return carry

    lax.fori_loop(1, 8, up_start, 0)
    prepare_up(tile)
    pltpu.make_async_copy(up_ref.at[tile], gbuf.at[pl.ds(1 + 2 * col, 2), :, rows], up_recv.at[tile]).start()

    def main_copy(other):
        to_tile, to_head = other // 4, other % 4
        src = send_ref.at[to_head * 10 + to_tile]
        dst = qkv.at[:, pl.ds(1 + 2 * head, 2), tile]
        return push(src, dst, main_send.at[other], main_recv.at[me], to_tile, to_head)

    def main_peer(place):
        turn = place // 4
        shift = 12 + ((turn + 1) // 2) * (2 * (turn % 2) - 1)
        return ((tile + shift) % 8) * 4 + (head + place) % 4

    def main_start(place, carry):
        other = main_peer(place)
        prepare((other % 4) * 10 + other // 4)
        main_copy(other).start()
        return carry

    lax.fori_loop(0, 16, main_start, 0)

    def ext_arrive(frame, carry):
        landing(qkv.at[:, pl.ds(11, 2), frame], ext_recv.at[frame]).wait()
        return carry

    lax.fori_loop(0, 8, ext_arrive, 0)

    def side_copy(side):
        source, target, step = ((12, 10, 1), (11, 13, -1))[side]
        return push(qkv.at[pl.ds(1, 2), source], qkv.at[pl.ds(1, 2), target],
                    side_send.at[side], side_recv.at[side], tile + step, head)

    @pl.when(col < 3)
    def _():
        side_copy(0).start()

    @pl.when(col > 0)
    def _():
        side_copy(1).start()

    lax.fori_loop(16, 28, main_start, 0)
    lax.fori_loop(29, 32, main_start, 0)
    prepare(head * 10 + tile)
    pltpu.make_async_copy(send_ref.at[head * 10 + tile], qkv.at[:, pl.ds(1 + 2 * head, 2), tile],
                          main_recv.at[me]).start()

    blank = jnp.zeros((FRAMES, 32, HEAD_DIM), jnp.bfloat16)
    for part in (1, 2):
        qkv[part, 0] = blank
        qkv[part, 9] = blank

        @pl.when(col == 0)
        def _(part=part):
            qkv[part, 10] = blank

        @pl.when(col == 3)
        def _(part=part):
            qkv[part, 13] = blank

    acc[...] = jnp.zeros_like(acc)

    scaling = HEAD_DIM ** (-0.5)
    key_at = lax.broadcasted_iota(jnp.int32, (768, 1), 0)

    def one_tile(job):
        first = job + 2 * (job // 8)
        low = jnp.where((job == 0) | ((job == 8) & (col == 0)), 256, 0)
        high = jnp.where((job == 7) | ((job == 9) & (col == 3)), 512, 768)
        usable = (key_at >= low) & (key_at < high)
        bias = jnp.where(usable, 0.0, -1e30)
        query = qkv[0, first + 1].reshape(256, HEAD_DIM)
        grad = gbuf[first + 1].reshape(256, HEAD_DIM)
        keys = qkv[1, pl.ds(first, 3)].reshape(768, HEAD_DIM)
        values = qkv[2, pl.ds(first, 3)].reshape(768, HEAD_DIM)
        scores = lax.dot_general(keys, query, (((1,), (1,)), ((), ())), preferred_element_type=jnp.float32)
        scores = scores * (scaling * math.log2(math.e)) + bias
        highest = jnp.max(scores, axis=0, keepdims=True)
        raised = jnp.exp2(scores - highest)
        weights = raised * (1.0 / jnp.sum(raised, axis=0, keepdims=True))
        weights_low = weights.astype(jnp.bfloat16)
        mixed = lax.dot_general(values, weights_low, (((0,), (0,)), ((), ())), preferred_element_type=jnp.float32)
        grad_across = grad.astype(jnp.float32).T
        offsets = jnp.sum(grad_across * mixed, axis=0, keepdims=True)
        weight_grad = lax.dot_general(values, grad, (((1,), (1,)), ((), ())), preferred_element_type=jnp.float32)
        score_low = (weights * (weight_grad - offsets)).astype(jnp.bfloat16)
        query_grad = lax.dot_general(keys, score_low, (((0,), (0,)), ((), ())), preferred_element_type=jnp.float32)
        obuf[0, first + 1] = mixed.T.astype(jnp.bfloat16).reshape(FRAMES, 32, HEAD_DIM)
        obuf[1, first + 1] = (query_grad * scaling).T.astype(jnp.bfloat16).reshape(FRAMES, 32, HEAD_DIM)
        key_terms = lax.dot_general(score_low, query, (((1,), (0,)), ((), ())), preferred_element_type=jnp.float32)
        value_terms = lax.dot_general(weights_low, grad, (((1,), (0,)), ((), ())), preferred_element_type=jnp.float32)
        acc[0, pl.ds(first, 3)] += (key_terms * scaling).reshape(3, 256, HEAD_DIM)
        acc[1, pl.ds(first, 3)] += value_terms.reshape(3, 256, HEAD_DIM)

    def settle(slot):
        for part in range(2):
            obuf[2 + part, slot] = acc[part, slot].astype(jnp.bfloat16).reshape(FRAMES, 32, HEAD_DIM)

    def out_piece(pair, other):
        return obuf.at[pl.ds(2 * pair, 2), pl.ds(1 + 2 * (other % 4), 2), :, pl.ds(16 * (other // 4), 16)]

    def out_copy(pair, other):
        return push(out_piece(pair, other), landed.at[pl.ds(2 * pair, 2), tile],
                    out_send.at[pair, other], out_recv.at[pair, tile], other, head)

    def out_start(pair, column):
        for step in (1, 0):
            other = 4 * ((row_half + step) % 2) + column

            @pl.when(other == tile)
            def _(other=other):
                pltpu.make_async_copy(out_piece(pair, other), landed.at[pl.ds(2 * pair, 2), tile],
                                      out_recv.at[pair, tile]).start()

            @pl.when(other != tile)
            def _(other=other):
                out_copy(pair, other).start()

    def outx_piece(pair, half):
        return obuf.at[pl.ds(2 * pair, 2), pl.ds(11, 2), :, pl.ds(16 * half, 16)]

    def outx_copy(pair, half):
        return push(outx_piece(pair, half), landed.at[pl.ds(2 * pair, 2), 8 + row_half],
                    outx_send.at[pair, half], outx_recv.at[pair, row_half], 4 * half + col, head)

    def outx_start(pair):
        for half in range(2):
            @pl.when(row_half == half)
            def _(half=half):
                pltpu.make_async_copy(outx_piece(pair, half), landed.at[pl.ds(2 * pair, 2), 8 + row_half],
                                      outx_recv.at[pair, row_half]).start()

            @pl.when(row_half != half)
            def _(half=half):
                outx_copy(pair, half).start()

    def rim_copy(side):
        slot, step = ((13, 1), (10, -1))[side]
        return push(obuf.at[pl.ds(2, 2), slot], rims.at[side], rim_send.at[side], rim_recv.at[side],
                    tile + step, head)

    @pl.when(col > 0)
    def _():
        landing(qkv.at[pl.ds(1, 2), 10], side_recv.at[0]).wait()

    @pl.when(col < 3)
    def _():
        landing(qkv.at[pl.ds(1, 2), 13], side_recv.at[1]).wait()

    for half in range(2):
        landing(gbuf.at[pl.ds(11, 2), :, pl.ds(16 * half, 16)], upx_recv.at[half]).wait()

    def ext_tile(job, carry):
        one_tile(job)
        return carry

    lax.fori_loop(8, 10, ext_tile, 0)
    settle(10)
    settle(13)

    @pl.when(col < 3)
    def _():
        rim_copy(0).start()

    @pl.when(col > 0)
    def _():
        rim_copy(1).start()

    outx_start(0)

    def finish_shared():
        @pl.when(col > 0)
        def _():
            landing(rims.at[0], rim_recv.at[0]).wait()
            for part in range(2):
                acc[part, 11] += rims[0, part].reshape(256, HEAD_DIM).astype(jnp.float32)

        @pl.when(col < 3)
        def _():
            landing(rims.at[1], rim_recv.at[1]).wait()
            for part in range(2):
                acc[part, 12] += rims[1, part].reshape(256, HEAD_DIM).astype(jnp.float32)

        settle(11)
        settle(12)
        outx_start(1)

    def main_arrive(other, carry):
        landing(qkv.at[:, pl.ds(1 + 2 * (other % 4), 2), other // 4], main_recv.at[other]).wait()
        return carry

    lax.fori_loop(0, 32, main_arrive, 0)

    def up_arrive(other, carry):
        landing(gbuf.at[pl.ds(1 + 2 * (other % 4), 2), :, pl.ds(16 * (other // 4), 16)], up_recv.at[other]).wait()
        return carry

    lax.fori_loop(0, 8, up_arrive, 0)
    def settle_column(column):
        settle(1 + 2 * column)
        settle(2 + 2 * column)
        out_start(1, column)

    def main_tile(step, carry):
        one_tile((step + 2 * col) % 8)

        @pl.when(step % 2 == 1)
        def _():
            out_start(0, (col + step // 2) % 4)

        @pl.when((step == 4) | (step == 6))
        def _():
            settle_column((col + step // 2 - 1) % 4)

        @pl.when(step == 3)
        def _():
            finish_shared()

        return carry

    lax.fori_loop(0, 8, main_tile, 0)
    settle_column((col + 3) % 4)
    settle_column(col)

    def place(ref, which, near, far):
        even, odd = regroup(near.reshape(16, 8, HEAD_DIM), far.reshape(16, 8, HEAD_DIM))
        ref[:, lanes(which)] = jnp.stack((even, odd), axis=1).reshape(256, HEAD_DIM).astype(jnp.bfloat16)

    out_refs = (attended_ref, query_ref, key_ref, value_ref)

    def wide(part, which, side):
        return landed[part, which, side].astype(jnp.float32)

    for pair in range(2):
        def out_arrive(step, carry, pair=pair):
            other = (tile + step) % 8
            landing(landed.at[pl.ds(2 * pair, 2), other], out_recv.at[pair, other]).wait()
            for part in (2 * pair, 2 * pair + 1):
                place(out_refs[part], other, wide(part, other, 0), wide(part, other, 1))
            return carry

        lax.fori_loop(0, 8, out_arrive, 0)
        for extra in range(2):
            landing(landed.at[pl.ds(2 * pair, 2), 8 + extra], outx_recv.at[pair, extra]).wait()
            for part in (2 * pair, 2 * pair + 1):
                place(out_refs[part], 8 + extra, wide(part, 8 + extra, 0), wide(part, 8 + extra, 1))

    def main_left(step, carry):
        main_copy((me + step) % 32).wait_send()
        return carry

    lax.fori_loop(1, 32, main_left, 0)

    def group_left(step, carry):
        up_copy((tile + step) % 8).wait_send()
        out_copy(0, (tile + step) % 8).wait_send()
        out_copy(1, (tile + step) % 8).wait_send()
        return carry

    lax.fori_loop(1, 8, group_left, 0)

    def ext_left(which, carry):
        @pl.when(jnp.logical_not(ext_is_own(which)))
        def _():
            ext_copy(which).wait_send()

        return carry

    lax.fori_loop(0, 8, ext_left, 0)
    for half in range(2):
        @pl.when(row_half != half)
        def _(half=half):
            upx_copy(half).wait_send()
            outx_copy(0, half).wait_send()
            outx_copy(1, half).wait_send()

    @pl.when(col < 3)
    def _():
        side_copy(0).wait_send()
        rim_copy(0).wait_send()

    @pl.when(col > 0)
    def _():
        side_copy(1).wait_send()
        rim_copy(1).wait_send()


def fast_local(query_slab, key_slab, value_slab, upstream):
    dma = pltpu.SemaphoreType.DMA
    out = pl.pallas_call(
        fast_kernel,
        out_shape=[jax.ShapeDtypeStruct((256, 10 * HEAD_DIM), jnp.bfloat16)] * 4,
        in_specs=[pl.BlockSpec(memory_space=pltpu.VMEM)] * 4,
        out_specs=[pl.BlockSpec(memory_space=pltpu.VMEM)] * 4,
        scratch_shapes=[
            pltpu.VMEM((40, 3, 2, 32, HEAD_DIM), jnp.bfloat16),
            pltpu.VMEM((10, 2, FRAMES, 16, HEAD_DIM), jnp.bfloat16),
            pltpu.VMEM((3, SLOTS, FRAMES, 32, HEAD_DIM), jnp.bfloat16),
            pltpu.VMEM((SLOTS, FRAMES, 32, HEAD_DIM), jnp.bfloat16),
            pltpu.VMEM((4, SLOTS, FRAMES, 32, HEAD_DIM), jnp.bfloat16),
            pltpu.VMEM((2, SLOTS, 256, HEAD_DIM), jnp.float32),
            pltpu.VMEM((4, 10, 2, FRAMES, 16, HEAD_DIM), jnp.bfloat16),
            pltpu.VMEM((2, 2, FRAMES, 32, HEAD_DIM), jnp.bfloat16),
            dma((32,)), dma((32,)), dma((8,)), dma((8,)), dma((2,)), dma((2,)),
            dma((8,)), dma((8,)), dma((2,)), dma((2,)), dma((2, 8)), dma((2, 8)), dma((2, 2)), dma((2, 2)),
            dma((2,)), dma((2,)),
        ],
        compiler_params=pltpu.CompilerParams(
            collective_id=0, has_side_effects=True, vmem_limit_bytes=48 * 1024 * 1024
        ),
        cost_estimate=pl.CostEstimate(flops=3 * 10**9, bytes_accessed=8 * 10**6, transcendentals=2 * 10**6),
    )(query_slab, key_slab, value_slab, upstream)
    return tuple(out)


def solution(mesh):
    placed = (
        P("tile", None, "head", None),
        P("tile", None, "head", None),
        P("tile", None, "head", None),
        P("tile", "head"),
    )

    def chosen(query_slab, key_slab, value_slab, upstream):
        two_rows = query_slab.shape == (4, 2, 8, 40 * HEAD_DIM) and upstream.shape == (256, 10 * HEAD_DIM)
        body = fast_local if two_rows and mesh.shape["tile"] == 8 and mesh.shape["head"] == 4 else local
        return body(query_slab, key_slab, value_slab, upstream)

    return jax.shard_map(
        chosen,
        mesh=mesh,
        in_specs=placed,
        out_specs=(P("tile", "head"), P("tile", "head"), P("tile", "head"), P("tile", "head")),
        check_vma=False,
    )
```

```python
import math

import jax
import jax.numpy as jnp
from jax import lax
from jax.experimental import pallas as pl
from jax.experimental.pallas import tpu as pltpu
from jax.sharding import PartitionSpec as P

HEAD_DIM = 128
FRAMES = 8
FRAME_W = 32
MESH = pl.DeviceIdType.MESH


masked_score = -1e30


def from_behind(value, axis, steps):
    count = lax.axis_size(axis)
    leading, last = (max(0, -steps), min(count, count - steps))
    return lax.ppermute(value, axis, [(source, source + steps) for source in range(leading, last)])


def to_tiles(grid, tile_rows, tile_cols):
    features = grid.shape[-1]
    shaped = grid.reshape(FRAMES, tile_rows, 4, tile_cols, 4, features)
    return shaped.transpose(1, 3, 0, 2, 4, 5).reshape(tile_rows, tile_cols, FRAMES * 16, features)


def from_tiles(tiles):
    tile_rows = tiles.shape[0]
    tile_cols = tiles.shape[1]
    features = tiles.shape[-1]
    shaped = tiles.reshape(tile_rows, tile_cols, FRAMES, 4, 4, features)
    return shaped.transpose(2, 0, 3, 1, 4, 5).reshape(FRAMES * tile_rows * tile_cols * 16, features)


def window_keys(nearby, tile_rows, tile_cols):
    features = nearby.shape[-1]
    shaped = nearby.reshape(2, FRAMES, tile_rows + 2, 4, tile_cols + 2, 4, features)
    pieces = [
        shaped[:, :, row_step : row_step + tile_rows, :, col_step : col_step + tile_cols]
        for row_step in range(3)
        for col_step in range(3)
    ]
    stacked = jnp.stack(pieces, axis=1)
    ordered = stacked.transpose(0, 3, 5, 1, 2, 4, 6, 7)
    return ordered.reshape(2, tile_rows, tile_cols, 144 * FRAMES, features)


def fold_keys(window, tile_rows, tile_cols):
    features = window.shape[-1]
    portions = window.reshape(tile_rows, tile_cols, 3, 3, FRAMES, 4, 4, features)
    accumulated = jnp.zeros((FRAMES, tile_rows + 2, 4, tile_cols + 2, 4, features), jnp.float32)
    for row_step in range(3):
        for col_step in range(3):
            portion = portions[:, :, row_step, col_step].transpose(2, 0, 3, 1, 4, 5)
            accumulated = accumulated.at[
                :, row_step : row_step + tile_rows, :, col_step : col_step + tile_cols
            ].add(portion)
    return accumulated.reshape(FRAMES, 4 * (tile_rows + 2), 4 * (tile_cols + 2), features)


def key_mask(tile_rows, tile_cols, row_first, col_first, rows_all, cols_all):
    row_index = jnp.arange(tile_rows, dtype=jnp.int32)[:, None, None, None]
    col_index = jnp.arange(tile_cols, dtype=jnp.int32)[None, :, None, None]
    row_steps = jnp.arange(3, dtype=jnp.int32)[None, None, :, None]
    col_steps = jnp.arange(3, dtype=jnp.int32)[None, None, None, :]
    row_place = row_first + row_index + row_steps - 1
    col_place = col_first + col_index + col_steps - 1
    usable = (row_place >= 0) & (row_place < rows_all) & (col_place >= 0) & (col_place < cols_all)
    spread = jnp.broadcast_to(usable[..., None], (tile_rows, tile_cols, 3, 3, FRAMES * 16))
    return spread.reshape(tile_rows, tile_cols, 144 * FRAMES)


def attend(query_blocks, key_window, value_window, grad_blocks, usable):
    tile_rows, pair_count, query_count, features = query_blocks.shape
    head_count = features // HEAD_DIM
    key_count = key_window.shape[2]
    query_heads = query_blocks.reshape(tile_rows, pair_count, query_count, head_count, HEAD_DIM)
    grad_heads = grad_blocks.reshape(tile_rows, pair_count, query_count, head_count, HEAD_DIM)
    key_heads = key_window.reshape(tile_rows, pair_count, key_count, head_count, HEAD_DIM)
    value_heads = value_window.reshape(tile_rows, pair_count, key_count, head_count, HEAD_DIM)
    scaling = HEAD_DIM ** (-0.5)
    scores = (
        jnp.einsum("rcqhd,rckhd->rchqk", query_heads, key_heads, preferred_element_type=jnp.float32)
        * scaling
    )
    scores = jnp.where(usable[:, :, None, None, :], scores, masked_score)
    highest = jnp.max(scores, axis=-1, keepdims=True)
    raised = jnp.exp(scores - highest)
    weights = raised / jnp.sum(raised, axis=-1, keepdims=True)
    weights_low = weights.astype(jnp.bfloat16)
    mixed = jnp.einsum(
        "rchqk,rckhd->rcqhd", weights_low, value_heads, preferred_element_type=jnp.float32
    )
    offsets = jnp.sum(grad_heads.astype(jnp.float32) * mixed, axis=-1).transpose(0, 1, 3, 2)
    weight_grad = jnp.einsum(
        "rcqhd,rckhd->rchqk", grad_heads, value_heads, preferred_element_type=jnp.float32
    )
    score_grad = weights * (weight_grad - offsets[..., None])
    score_low = score_grad.astype(jnp.bfloat16)
    query_grad = (
        jnp.einsum("rchqk,rckhd->rcqhd", score_low, key_heads, preferred_element_type=jnp.float32)
        * scaling
    )
    key_terms = (
        jnp.einsum("rchqk,rcqhd->rckhd", score_low, query_heads, preferred_element_type=jnp.float32)
        * scaling
    )
    value_terms = jnp.einsum(
        "rchqk,rcqhd->rckhd", weights_low, grad_heads, preferred_element_type=jnp.float32
    )
    return (
        mixed.reshape(tile_rows, pair_count, query_count, features),
        query_grad.reshape(tile_rows, pair_count, query_count, features),
        key_terms.reshape(tile_rows, pair_count, key_count, features),
        value_terms.reshape(tile_rows, pair_count, key_count, features),
    )


def pass_keys(block, step):
    return from_behind(block, "tile", step)


def pass_terms(block, step):
    return from_behind(block, "tile", step)


def settle(received):
    rows_here = received.shape[-3]
    width_here = received.shape[-2]
    features = received.shape[-1]
    shaped = received.reshape(FRAMES, 4, rows_here, width_here, features).transpose(0, 2, 1, 3, 4)
    return shaped.reshape(FRAMES, 4 * rows_here, width_here, features)


def local(query_slab, key_slab, value_slab, upstream):
    query_rows, key_rows, value_rows = (
        lax.all_to_all(query_slab, "head", split_axis=3, concat_axis=2, tiled=True),
        lax.all_to_all(key_slab, "head", split_axis=3, concat_axis=2, tiled=True),
        lax.all_to_all(value_slab, "head", split_axis=3, concat_axis=2, tiled=True),
    )
    owner_count = lax.axis_size("tile")
    row_groups = owner_count // 4
    source_count = query_rows.shape[0]
    features = query_rows.shape[3]
    tile_rows = query_rows.shape[1] // row_groups
    tile_cols = FRAME_W // 16
    band_width = 4 * tile_cols
    line_count = 4 * tile_rows
    owner_index = lax.axis_index("tile")
    row_group = owner_index // 4
    col_group = owner_index % 4
    left_ok = col_group > 0
    right_ok = col_group < 3

    def to_owners(slab):
        shaped = slab.reshape(source_count, row_groups, tile_rows, 4, band_width, features)
        return shaped.transpose(1, 3, 0, 2, 4, 5).reshape(
            owner_count, source_count, tile_rows, band_width, features
        )

    query_got, key_got, value_got = (
        lax.all_to_all(to_owners(query_rows), "tile", split_axis=0, concat_axis=1, tiled=True),
        lax.all_to_all(to_owners(key_rows), "tile", split_axis=0, concat_axis=1, tiled=True),
        lax.all_to_all(to_owners(value_rows), "tile", split_axis=0, concat_axis=1, tiled=True),
    )
    owned_query = settle(query_got)
    owned_pair = jnp.stack((settle(key_got), settle(value_got)))
    from_left = pass_keys(owned_pair[:, :, :, band_width - 4 :], 1)
    from_right = pass_keys(owned_pair[:, :, :, 0:4], -1)
    from_left = jnp.where(left_ok, from_left, jnp.zeros_like(from_left))
    from_right = jnp.where(right_ok, from_right, jnp.zeros_like(from_right))
    wide_pair = jnp.concatenate((from_left, owned_pair, from_right), axis=3)
    from_above = pass_keys(wide_pair, 4)
    from_below = pass_keys(wide_pair, -4)
    nearby = jnp.concatenate((from_above, wide_pair, from_below), axis=2)
    query_tiles = to_tiles(owned_query, tile_rows, tile_cols)
    grad_tiles = to_tiles(
        upstream.reshape(FRAMES, line_count, band_width, features), tile_rows, tile_cols
    )
    usable = key_mask(
        tile_rows,
        tile_cols,
        row_group * tile_rows,
        col_group * tile_cols,
        row_groups * tile_rows,
        4 * tile_cols,
    )
    totals = jnp.zeros((2, FRAMES, line_count + 8, band_width + 8, features), jnp.float32)

    def one_column(totals, column):
        first_col = column * 4
        nearby_part = lax.dynamic_slice_in_dim(nearby, first_col, 12, 3)
        windows = window_keys(nearby_part, tile_rows, 1)
        query_part = lax.dynamic_slice_in_dim(query_tiles, column, 1, 1)
        grad_part = lax.dynamic_slice_in_dim(grad_tiles, column, 1, 1)
        usable_part = lax.dynamic_slice_in_dim(usable, column, 1, 1)
        mixed, query_grad, key_terms, value_terms = attend(
            query_part, windows[0], windows[1], grad_part, usable_part
        )
        folded = jnp.stack(
            (fold_keys(key_terms, tile_rows, 1), fold_keys(value_terms, tile_rows, 1))
        )
        current = lax.dynamic_slice_in_dim(totals, first_col, 12, 3)
        totals = lax.dynamic_update_slice_in_dim(totals, current + folded, first_col, 3)
        return (totals, (mixed[:, 0].astype(jnp.bfloat16), query_grad[:, 0].astype(jnp.bfloat16)))

    extended, (mixed, query_grad) = lax.scan(
        one_column, totals, jnp.arange(tile_cols, dtype=jnp.int32)
    )
    attended = from_tiles(jnp.swapaxes(mixed, 0, 1))
    query_out = from_tiles(jnp.swapaxes(query_grad, 0, 1))
    top_band = extended[:, :, 0:4].astype(jnp.bfloat16)
    bottom_band = extended[:, :, line_count + 4 :].astype(jnp.bfloat16)
    terms_below = pass_terms(top_band, -4).astype(jnp.float32)
    terms_above = pass_terms(bottom_band, 4).astype(jnp.float32)
    incoming = terms_above
    incoming = incoming + terms_below
    rowed = extended[:, :, 4 : line_count + 4] + incoming
    left_terms = rowed[:, :, :, 0:4].astype(jnp.bfloat16)
    right_terms = rowed[:, :, :, band_width + 4 :].astype(jnp.bfloat16)
    terms_right = pass_terms(left_terms, -1)
    terms_left = pass_terms(right_terms, 1)
    terms_right = jnp.where(right_ok, terms_right, jnp.zeros_like(terms_right)).astype(jnp.float32)
    terms_left = jnp.where(left_ok, terms_left, jnp.zeros_like(terms_left)).astype(jnp.float32)
    summed = rowed[:, :, :, 4 : band_width + 4]
    summed = summed + jnp.pad(terms_left, ((0, 0), (0, 0), (0, 0), (0, band_width - 4), (0, 0)))
    summed = summed + jnp.pad(terms_right, ((0, 0), (0, 0), (0, 0), (band_width - 4, 0), (0, 0)))
    summed = summed.astype(jnp.bfloat16)
    key_grad = summed[0].reshape(-1, features)
    value_grad = summed[1].reshape(-1, features)
    return (attended, query_out, key_grad, value_grad)


SLOTS = 14


def fast_kernel(query_hbm, key_hbm, value_hbm, grad_hbm, attended_ref, query_ref, key_ref, value_ref,
                slabs, grad_in, results, send_ref, up_ref, qkv, gbuf, obuf, acc, landed, rims,
                main_send, main_recv, ext_send, ext_recv, side_send, side_recv,
                up_send, up_recv, upx_send, upx_recv, out_send, out_recv, outx_send, outx_recv,
                rim_send, rim_recv, slab_sem, grad_sem, done_sem):
    tile = lax.axis_index("tile")
    head = lax.axis_index("head")
    me = tile * 4 + head
    row_half = tile // 4
    col = tile % 4

    def slab_copy(part, group):
        lanes_of = pl.ds(group * 10 * HEAD_DIM, 10 * HEAD_DIM)
        source = (query_hbm, key_hbm, value_hbm)[part]
        return pltpu.make_async_copy(source.at[:, :, :, lanes_of], slabs.at[part, :, :, :, lanes_of],
                                     slab_sem.at[part, group])

    def grad_copy(quarter):
        rows_of = pl.ds(64 * quarter, 64)
        return pltpu.make_async_copy(grad_hbm.at[rows_of], grad_in.at[rows_of], grad_sem.at[quarter])

    for group in range(4):
        for part in range(3):
            slab_copy(part, group).start()
    for quarter in range(4):
        grad_copy(quarter).start()

    barrier = pltpu.get_barrier_semaphore()

    def greet(step, carry):
        other = (me + step) % 32
        pl.semaphore_signal(barrier, inc=1, device_id=(other // 4, other % 4), device_id_type=MESH)
        return carry

    lax.fori_loop(1, 32, greet, 0)

    def regroup(first, second):
        upper = lax.broadcasted_iota(jnp.int32, first.shape, first.ndim - 2) < 4
        near = jnp.where(upper, first, pltpu.roll(second, 4, first.ndim - 2))
        far = jnp.where(upper, pltpu.roll(first, 4, first.ndim - 2), second)
        return near, far

    def lanes(which):
        return pl.ds(pl.multiple_of(which * HEAD_DIM, HEAD_DIM), HEAD_DIM)

    def prepare(which):
        for part in range(3):
            lines = slabs[part, :, :, :, lanes(which)].astype(jnp.float32).reshape(2, 2, 16, HEAD_DIM)
            first = lines[:, 0].reshape(4, 8, HEAD_DIM)
            second = lines[:, 1].reshape(4, 8, HEAD_DIM)
            for side, taken in enumerate(regroup(first, second)):
                ordered = jnp.stack((taken[0], taken[2], taken[1], taken[3])).reshape(32, HEAD_DIM)
                send_ref[which, part, side] = ordered.astype(jnp.bfloat16)

    def prepare_up(which):
        lines = grad_in[:, lanes(which)].astype(jnp.float32).reshape(16, 2, 8, HEAD_DIM)
        for side, taken in enumerate(regroup(lines[:, 0], lines[:, 1])):
            up_ref[which, side] = taken.reshape(FRAMES, 16, HEAD_DIM).astype(jnp.bfloat16)

    def prepare_shared(which, carry):
        prepare((which // 2) * 10 + 8 + which % 2)
        return carry

    for group in range(4):
        for part in range(3):
            slab_copy(part, group).wait()
    lax.fori_loop(0, 8, prepare_shared, 0)
    pl.semaphore_wait(barrier, 31)

    def push(src, dst, send_sem, recv_sem, to_tile, to_head):
        return pltpu.make_async_remote_copy(
            src_ref=src, dst_ref=dst, send_sem=send_sem, recv_sem=recv_sem,
            device_id=(to_tile, to_head), device_id_type=MESH)

    def landing(dst, recv_sem):
        return pltpu.make_async_copy(dst, dst, recv_sem)

    rows = pl.ds(16 * row_half, 16)

    def ext_parts(which):
        to_head, extra = which // 2, which % 2
        return to_head, extra, to_head * 10 + 8 + extra

    def ext_copy(which):
        to_head, extra, source = ext_parts(which)
        return push(send_ref.at[source], qkv.at[:, pl.ds(11, 2), tile],
                    ext_send.at[which], ext_recv.at[tile], 4 * extra + head, to_head)

    def ext_is_own(which):
        to_head, extra, source = ext_parts(which)
        return (4 * extra + head) * 4 + to_head == me

    def ext_start(which, carry):
        to_head, extra, source = ext_parts(which)

        @pl.when(ext_is_own(which))
        def _():
            pltpu.make_async_copy(send_ref.at[source], qkv.at[:, pl.ds(11, 2), tile], ext_recv.at[tile]).start()

        @pl.when(jnp.logical_not(ext_is_own(which)))
        def _():
            ext_copy(which).start()

        return carry

    lax.fori_loop(0, 8, ext_start, 0)

    def upx_copy(extra):
        return push(up_ref.at[8 + extra], gbuf.at[pl.ds(11, 2), :, rows],
                    upx_send.at[extra], upx_recv.at[row_half], 4 * extra + col, head)

    for quarter in range(4):
        grad_copy(quarter).wait()
    for extra in range(2):
        prepare_up(8 + extra)

        @pl.when(row_half == extra)
        def _(extra=extra):
            pltpu.make_async_copy(up_ref.at[8 + extra], gbuf.at[pl.ds(11, 2), :, rows],
                                  upx_recv.at[row_half]).start()

        @pl.when(row_half != extra)
        def _(extra=extra):
            upx_copy(extra).start()

    def up_copy(other):
        return push(up_ref.at[other], gbuf.at[pl.ds(1 + 2 * col, 2), :, rows],
                    up_send.at[other], up_recv.at[tile], other, head)

    def up_start(step, carry):
        other = (tile + 3 + step + step // 5) % 8
        prepare_up(other)
        up_copy(other).start()
        return carry

    lax.fori_loop(1, 8, up_start, 0)
    prepare_up(tile)
    pltpu.make_async_copy(up_ref.at[tile], gbuf.at[pl.ds(1 + 2 * col, 2), :, rows], up_recv.at[tile]).start()

    def main_copy(other):
        to_tile, to_head = other // 4, other % 4
        src = send_ref.at[to_head * 10 + to_tile]
        dst = qkv.at[:, pl.ds(1 + 2 * head, 2), tile]
        return push(src, dst, main_send.at[other], main_recv.at[me], to_tile, to_head)

    def main_peer(place):
        turn = place // 8
        column = (head + turn + turn // 2 - 2 * (turn // 3)) % 4
        other_tile = 4 * ((row_half + 1 - (place % 8) // 4) % 2) + column
        return other_tile * 4 + (head + place) % 4

    def main_start(place, carry):
        other = main_peer(place)
        prepare((other % 4) * 10 + other // 4)

        @pl.when(other != me)
        def _():
            main_copy(other).start()

        @pl.when(other == me)
        def _():
            pltpu.make_async_copy(send_ref.at[head * 10 + tile], qkv.at[:, pl.ds(1 + 2 * head, 2), tile],
                                  main_recv.at[me]).start()

        return carry

    lax.fori_loop(0, 16, main_start, 0)

    def ext_arrive(frame, carry):
        landing(qkv.at[:, pl.ds(11, 2), frame], ext_recv.at[frame]).wait()
        return carry

    lax.fori_loop(0, 8, ext_arrive, 0)

    def side_copy(side):
        source, target, step = ((12, 10, 1), (11, 13, -1))[side]
        return push(qkv.at[pl.ds(1, 2), source], qkv.at[pl.ds(1, 2), target],
                    side_send.at[side], side_recv.at[side], tile + step, head)

    @pl.when(col < 3)
    def _():
        side_copy(0).start()

    @pl.when(col > 0)
    def _():
        side_copy(1).start()

    lax.fori_loop(16, 32, main_start, 0)

    blank = jnp.zeros((FRAMES, 32, HEAD_DIM), jnp.bfloat16)
    for part in (1, 2):
        qkv[part, 0] = blank
        qkv[part, 9] = blank

        @pl.when(col == 0)
        def _(part=part):
            qkv[part, 10] = blank

        @pl.when(col == 3)
        def _(part=part):
            qkv[part, 13] = blank

    acc[...] = jnp.zeros_like(acc)

    scaling = HEAD_DIM ** (-0.5)
    key_at = lax.broadcasted_iota(jnp.int32, (768, 1), 0)

    def one_tile(job):
        first = job + 2 * (job // 8)
        low = jnp.where((job == 0) | ((job == 8) & (col == 0)), 256, 0)
        high = jnp.where((job == 7) | ((job == 9) & (col == 3)), 512, 768)
        usable = (key_at >= low) & (key_at < high)
        bias = jnp.where(usable, 0.0, -1e30)
        query = qkv[0, first + 1].reshape(256, HEAD_DIM)
        grad = gbuf[first + 1].reshape(256, HEAD_DIM)
        keys = qkv[1, pl.ds(first, 3)].reshape(768, HEAD_DIM)
        values = qkv[2, pl.ds(first, 3)].reshape(768, HEAD_DIM)
        scores = lax.dot_general(keys, query, (((1,), (1,)), ((), ())), preferred_element_type=jnp.float32)
        scores = scores * (scaling * math.log2(math.e)) + bias
        highest = jnp.max(scores, axis=0, keepdims=True)
        raised = jnp.exp2(scores - highest)
        weights = raised * (1.0 / jnp.sum(raised, axis=0, keepdims=True))
        weights_low = weights.astype(jnp.bfloat16)
        mixed = lax.dot_general(values, weights_low, (((0,), (0,)), ((), ())), preferred_element_type=jnp.float32)
        grad_across = grad.astype(jnp.float32).T
        offsets = jnp.sum(grad_across * mixed, axis=0, keepdims=True)
        weight_grad = lax.dot_general(values, grad, (((1,), (1,)), ((), ())), preferred_element_type=jnp.float32)
        score_low = (weights * (weight_grad - offsets)).astype(jnp.bfloat16)
        query_grad = lax.dot_general(keys, score_low, (((0,), (0,)), ((), ())), preferred_element_type=jnp.float32)
        obuf[0, first + 1] = mixed.T.astype(jnp.bfloat16).reshape(FRAMES, 32, HEAD_DIM)
        obuf[1, first + 1] = (query_grad * scaling).T.astype(jnp.bfloat16).reshape(FRAMES, 32, HEAD_DIM)
        key_terms = lax.dot_general(score_low, query, (((1,), (0,)), ((), ())), preferred_element_type=jnp.float32)
        value_terms = lax.dot_general(weights_low, grad, (((1,), (0,)), ((), ())), preferred_element_type=jnp.float32)
        acc[0, pl.ds(first, 3)] += (key_terms * scaling).reshape(3, 256, HEAD_DIM)
        acc[1, pl.ds(first, 3)] += value_terms.reshape(3, 256, HEAD_DIM)

    def settle(slot):
        for part in range(2):
            obuf[2 + part, slot] = acc[part, slot].astype(jnp.bfloat16).reshape(FRAMES, 32, HEAD_DIM)

    def out_piece(pair, other):
        return obuf.at[pl.ds(2 * pair, 2), pl.ds(1 + 2 * (other % 4), 2), :, pl.ds(16 * (other // 4), 16)]

    def out_copy(pair, other):
        return push(out_piece(pair, other), landed.at[pl.ds(2 * pair, 2), tile],
                    out_send.at[pair, other], out_recv.at[pair, tile], other, head)

    def out_start(pair, column):
        for step in (1, 0):
            other = 4 * ((row_half + step) % 2) + column

            @pl.when(other == tile)
            def _(other=other):
                pltpu.make_async_copy(out_piece(pair, other), landed.at[pl.ds(2 * pair, 2), tile],
                                      out_recv.at[pair, tile]).start()

            @pl.when(other != tile)
            def _(other=other):
                out_copy(pair, other).start()

    def outx_piece(pair, half):
        return obuf.at[pl.ds(2 * pair, 2), pl.ds(11, 2), :, pl.ds(16 * half, 16)]

    def outx_copy(pair, half):
        return push(outx_piece(pair, half), landed.at[pl.ds(2 * pair, 2), 8 + row_half],
                    outx_send.at[pair, half], outx_recv.at[pair, row_half], 4 * half + col, head)

    def outx_start(pair):
        for half in range(2):
            @pl.when(row_half == half)
            def _(half=half):
                pltpu.make_async_copy(outx_piece(pair, half), landed.at[pl.ds(2 * pair, 2), 8 + row_half],
                                      outx_recv.at[pair, row_half]).start()

            @pl.when(row_half != half)
            def _(half=half):
                outx_copy(pair, half).start()

    def rim_copy(side):
        slot, step = ((13, 1), (10, -1))[side]
        return push(obuf.at[pl.ds(2, 2), slot], rims.at[side], rim_send.at[side], rim_recv.at[side],
                    tile + step, head)

    @pl.when(col > 0)
    def _():
        landing(qkv.at[pl.ds(1, 2), 10], side_recv.at[0]).wait()

    @pl.when(col < 3)
    def _():
        landing(qkv.at[pl.ds(1, 2), 13], side_recv.at[1]).wait()

    for half in range(2):
        landing(gbuf.at[pl.ds(11, 2), :, pl.ds(16 * half, 16)], upx_recv.at[half]).wait()

    def ext_tile(job, carry):
        one_tile(job)
        return carry

    lax.fori_loop(8, 10, ext_tile, 0)
    settle(10)
    settle(13)

    @pl.when(col < 3)
    def _():
        rim_copy(0).start()

    @pl.when(col > 0)
    def _():
        rim_copy(1).start()

    outx_start(0)

    def finish_shared():
        @pl.when(col > 0)
        def _():
            landing(rims.at[0], rim_recv.at[0]).wait()
            for part in range(2):
                acc[part, 11] += rims[0, part].reshape(256, HEAD_DIM).astype(jnp.float32)

        @pl.when(col < 3)
        def _():
            landing(rims.at[1], rim_recv.at[1]).wait()
            for part in range(2):
                acc[part, 12] += rims[1, part].reshape(256, HEAD_DIM).astype(jnp.float32)

        settle(11)
        settle(12)
        outx_start(1)

    def main_arrive(place, carry):
        column = (col + 3 + place // 8) % 4
        frame = place % 8
        landing(qkv.at[:, pl.ds(1 + 2 * column, 2), frame], main_recv.at[frame * 4 + column]).wait()
        return carry

    lax.fori_loop(0, 24, main_arrive, 0)

    def up_arrive(other, carry):
        landing(gbuf.at[pl.ds(1 + 2 * (other % 4), 2), :, pl.ds(16 * (other // 4), 16)], up_recv.at[other]).wait()
        return carry

    lax.fori_loop(0, 8, up_arrive, 0)
    def settle_column(column):
        settle(1 + 2 * column)
        settle(2 + 2 * column)
        out_start(1, column)

    def main_tile(step, carry):
        @pl.when(step == 3)
        def _():
            lax.fori_loop(24, 32, main_arrive, 0)

        one_tile((step + 2 * col) % 8)

        @pl.when(step % 2 == 1)
        def _():
            out_start(0, (col + step // 2) % 4)

        @pl.when((step == 4) | (step == 6))
        def _():
            settle_column((col + step // 2 - 1) % 4)

        @pl.when(step == 3)
        def _():
            finish_shared()

        return carry

    lax.fori_loop(0, 8, main_tile, 0)
    settle_column((col + 3) % 4)
    settle_column(col)

    out_refs = (attended_ref, query_ref, key_ref, value_ref)

    def result_copy(part, which):
        return pltpu.make_async_copy(results.at[part, :, lanes(which)], out_refs[part].at[:, lanes(which)],
                                     done_sem.at[part, which])

    def place(part, which, near, far):
        even, odd = regroup(near.reshape(16, 8, HEAD_DIM), far.reshape(16, 8, HEAD_DIM))
        lines = jnp.stack((even, odd), axis=1).reshape(256, HEAD_DIM)
        results[part, :, lanes(which)] = lines.astype(jnp.bfloat16)
        result_copy(part, which).start()

    def wide(part, which, side):
        return landed[part, which, side].astype(jnp.float32)

    for pair in range(2):
        def out_arrive(step, carry, pair=pair):
            other = (tile + step) % 8
            landing(landed.at[pl.ds(2 * pair, 2), other], out_recv.at[pair, other]).wait()
            for part in (2 * pair, 2 * pair + 1):
                place(part, other, wide(part, other, 0), wide(part, other, 1))
            return carry

        lax.fori_loop(0, 8, out_arrive, 0)
        for extra in range(2):
            landing(landed.at[pl.ds(2 * pair, 2), 8 + extra], outx_recv.at[pair, extra]).wait()
            for part in (2 * pair, 2 * pair + 1):
                place(part, 8 + extra, wide(part, 8 + extra, 0), wide(part, 8 + extra, 1))

    def results_done(which, carry):
        for part in range(4):
            result_copy(part, which).wait()
        return carry

    lax.fori_loop(0, 10, results_done, 0)

    def main_left(step, carry):
        main_copy((me + step) % 32).wait_send()
        return carry

    lax.fori_loop(1, 32, main_left, 0)

    def group_left(step, carry):
        up_copy((tile + step) % 8).wait_send()
        out_copy(0, (tile + step) % 8).wait_send()
        out_copy(1, (tile + step) % 8).wait_send()
        return carry

    lax.fori_loop(1, 8, group_left, 0)

    def ext_left(which, carry):
        @pl.when(jnp.logical_not(ext_is_own(which)))
        def _():
            ext_copy(which).wait_send()

        return carry

    lax.fori_loop(0, 8, ext_left, 0)
    for half in range(2):
        @pl.when(row_half != half)
        def _(half=half):
            upx_copy(half).wait_send()
            outx_copy(0, half).wait_send()
            outx_copy(1, half).wait_send()

    @pl.when(col < 3)
    def _():
        side_copy(0).wait_send()
        rim_copy(0).wait_send()

    @pl.when(col > 0)
    def _():
        side_copy(1).wait_send()
        rim_copy(1).wait_send()


def write_kernel(*refs):
    sources, targets, sems = refs[:4], refs[4:8], refs[8]
    copies = [
        pltpu.make_async_copy(
            sources[part].at[pl.ds(64 * quarter, 64)], targets[part].at[pl.ds(64 * quarter, 64)], sems.at[part, quarter]
        )
        for quarter in range(4)
        for part in range(4)
    ]
    for copy in copies:
        copy.start()
    for copy in copies:
        copy.wait()


def fast_local(query_slab, key_slab, value_slab, upstream):
    dma = pltpu.SemaphoreType.DMA
    out = pl.pallas_call(
        fast_kernel,
        out_shape=[jax.ShapeDtypeStruct((256, 10 * HEAD_DIM), jnp.bfloat16)] * 4,
        in_specs=[pl.BlockSpec(memory_space=pltpu.HBM)] * 4,
        out_specs=[pl.BlockSpec(memory_space=pltpu.HBM)] * 4,
        scratch_shapes=[
            pltpu.VMEM((3, 4, 2, 8, 40 * HEAD_DIM), jnp.bfloat16),
            pltpu.VMEM((256, 10 * HEAD_DIM), jnp.bfloat16),
            pltpu.VMEM((4, 256, 10 * HEAD_DIM), jnp.bfloat16),
            pltpu.VMEM((40, 3, 2, 32, HEAD_DIM), jnp.bfloat16),
            pltpu.VMEM((10, 2, FRAMES, 16, HEAD_DIM), jnp.bfloat16),
            pltpu.VMEM((3, SLOTS, FRAMES, 32, HEAD_DIM), jnp.bfloat16),
            pltpu.VMEM((SLOTS, FRAMES, 32, HEAD_DIM), jnp.bfloat16),
            pltpu.VMEM((4, SLOTS, FRAMES, 32, HEAD_DIM), jnp.bfloat16),
            pltpu.VMEM((2, SLOTS, 256, HEAD_DIM), jnp.float32),
            pltpu.VMEM((4, 10, 2, FRAMES, 16, HEAD_DIM), jnp.bfloat16),
            pltpu.VMEM((2, 2, FRAMES, 32, HEAD_DIM), jnp.bfloat16),
            dma((32,)), dma((32,)), dma((8,)), dma((8,)), dma((2,)), dma((2,)),
            dma((8,)), dma((8,)), dma((2,)), dma((2,)), dma((2, 8)), dma((2, 8)), dma((2, 2)), dma((2, 2)),
            dma((2,)), dma((2,)), dma((3, 4)), dma((4,)), dma((4, 10)),
        ],
        compiler_params=pltpu.CompilerParams(
            collective_id=0, has_side_effects=True, vmem_limit_bytes=61 * 1024 * 1024
        ),
        cost_estimate=pl.CostEstimate(flops=3 * 10**9, bytes_accessed=8 * 10**6, transcendentals=2 * 10**6),
    )(query_slab, key_slab, value_slab, upstream)
    return tuple(
        pl.pallas_call(
            write_kernel,
            out_shape=[jax.ShapeDtypeStruct((256, 10 * HEAD_DIM), jnp.bfloat16)] * 4,
            in_specs=[pl.BlockSpec(memory_space=pltpu.HBM)] * 4,
            out_specs=[pl.BlockSpec(memory_space=pltpu.HBM)] * 4,
            scratch_shapes=[dma((4, 4))],
            compiler_params=pltpu.CompilerParams(vmem_limit_bytes=61 * 1024 * 1024),
            cost_estimate=pl.CostEstimate(flops=0, bytes_accessed=5 * 10**6, transcendentals=0),
        )(*out)
    )


def solution(mesh):
    placed = (
        P("tile", None, "head", None),
        P("tile", None, "head", None),
        P("tile", None, "head", None),
        P("tile", "head"),
    )

    def chosen(query_slab, key_slab, value_slab, upstream):
        two_rows = query_slab.shape == (4, 2, 8, 40 * HEAD_DIM) and upstream.shape == (256, 10 * HEAD_DIM)
        body = fast_local if two_rows and mesh.shape["tile"] == 8 and mesh.shape["head"] == 4 else local
        return body(query_slab, key_slab, value_slab, upstream)

    return jax.shard_map(
        chosen,
        mesh=mesh,
        in_specs=placed,
        out_specs=(P("tile", "head"), P("tile", "head"), P("tile", "head"), P("tile", "head")),
        check_vma=False,
    )
```

```python
import math

import jax
import jax.numpy as jnp
from jax import lax
from jax.experimental import pallas as pl
from jax.experimental.pallas import tpu as pltpu
from jax.sharding import PartitionSpec as P

HEAD_DIM = 128
FRAMES = 8
FRAME_W = 32
MESH = pl.DeviceIdType.MESH


masked_score = -1e30


def from_behind(value, axis, steps):
    count = lax.axis_size(axis)
    leading, last = (max(0, -steps), min(count, count - steps))
    return lax.ppermute(value, axis, [(source, source + steps) for source in range(leading, last)])


def to_tiles(grid, tile_rows, tile_cols):
    features = grid.shape[-1]
    shaped = grid.reshape(FRAMES, tile_rows, 4, tile_cols, 4, features)
    return shaped.transpose(1, 3, 0, 2, 4, 5).reshape(tile_rows, tile_cols, FRAMES * 16, features)


def from_tiles(tiles):
    tile_rows = tiles.shape[0]
    tile_cols = tiles.shape[1]
    features = tiles.shape[-1]
    shaped = tiles.reshape(tile_rows, tile_cols, FRAMES, 4, 4, features)
    return shaped.transpose(2, 0, 3, 1, 4, 5).reshape(FRAMES * tile_rows * tile_cols * 16, features)


def window_keys(nearby, tile_rows, tile_cols):
    features = nearby.shape[-1]
    shaped = nearby.reshape(2, FRAMES, tile_rows + 2, 4, tile_cols + 2, 4, features)
    pieces = [
        shaped[:, :, row_step : row_step + tile_rows, :, col_step : col_step + tile_cols]
        for row_step in range(3)
        for col_step in range(3)
    ]
    stacked = jnp.stack(pieces, axis=1)
    ordered = stacked.transpose(0, 3, 5, 1, 2, 4, 6, 7)
    return ordered.reshape(2, tile_rows, tile_cols, 144 * FRAMES, features)


def fold_keys(window, tile_rows, tile_cols):
    features = window.shape[-1]
    portions = window.reshape(tile_rows, tile_cols, 3, 3, FRAMES, 4, 4, features)
    accumulated = jnp.zeros((FRAMES, tile_rows + 2, 4, tile_cols + 2, 4, features), jnp.float32)
    for row_step in range(3):
        for col_step in range(3):
            portion = portions[:, :, row_step, col_step].transpose(2, 0, 3, 1, 4, 5)
            accumulated = accumulated.at[
                :, row_step : row_step + tile_rows, :, col_step : col_step + tile_cols
            ].add(portion)
    return accumulated.reshape(FRAMES, 4 * (tile_rows + 2), 4 * (tile_cols + 2), features)


def key_mask(tile_rows, tile_cols, row_first, col_first, rows_all, cols_all):
    row_index = jnp.arange(tile_rows, dtype=jnp.int32)[:, None, None, None]
    col_index = jnp.arange(tile_cols, dtype=jnp.int32)[None, :, None, None]
    row_steps = jnp.arange(3, dtype=jnp.int32)[None, None, :, None]
    col_steps = jnp.arange(3, dtype=jnp.int32)[None, None, None, :]
    row_place = row_first + row_index + row_steps - 1
    col_place = col_first + col_index + col_steps - 1
    usable = (row_place >= 0) & (row_place < rows_all) & (col_place >= 0) & (col_place < cols_all)
    spread = jnp.broadcast_to(usable[..., None], (tile_rows, tile_cols, 3, 3, FRAMES * 16))
    return spread.reshape(tile_rows, tile_cols, 144 * FRAMES)


def attend(query_blocks, key_window, value_window, grad_blocks, usable):
    tile_rows, pair_count, query_count, features = query_blocks.shape
    head_count = features // HEAD_DIM
    key_count = key_window.shape[2]
    query_heads = query_blocks.reshape(tile_rows, pair_count, query_count, head_count, HEAD_DIM)
    grad_heads = grad_blocks.reshape(tile_rows, pair_count, query_count, head_count, HEAD_DIM)
    key_heads = key_window.reshape(tile_rows, pair_count, key_count, head_count, HEAD_DIM)
    value_heads = value_window.reshape(tile_rows, pair_count, key_count, head_count, HEAD_DIM)
    scaling = HEAD_DIM ** (-0.5)
    scores = (
        jnp.einsum("rcqhd,rckhd->rchqk", query_heads, key_heads, preferred_element_type=jnp.float32)
        * scaling
    )
    scores = jnp.where(usable[:, :, None, None, :], scores, masked_score)
    highest = jnp.max(scores, axis=-1, keepdims=True)
    raised = jnp.exp(scores - highest)
    weights = raised / jnp.sum(raised, axis=-1, keepdims=True)
    weights_low = weights.astype(jnp.bfloat16)
    mixed = jnp.einsum(
        "rchqk,rckhd->rcqhd", weights_low, value_heads, preferred_element_type=jnp.float32
    )
    offsets = jnp.sum(grad_heads.astype(jnp.float32) * mixed, axis=-1).transpose(0, 1, 3, 2)
    weight_grad = jnp.einsum(
        "rcqhd,rckhd->rchqk", grad_heads, value_heads, preferred_element_type=jnp.float32
    )
    score_grad = weights * (weight_grad - offsets[..., None])
    score_low = score_grad.astype(jnp.bfloat16)
    query_grad = (
        jnp.einsum("rchqk,rckhd->rcqhd", score_low, key_heads, preferred_element_type=jnp.float32)
        * scaling
    )
    key_terms = (
        jnp.einsum("rchqk,rcqhd->rckhd", score_low, query_heads, preferred_element_type=jnp.float32)
        * scaling
    )
    value_terms = jnp.einsum(
        "rchqk,rcqhd->rckhd", weights_low, grad_heads, preferred_element_type=jnp.float32
    )
    return (
        mixed.reshape(tile_rows, pair_count, query_count, features),
        query_grad.reshape(tile_rows, pair_count, query_count, features),
        key_terms.reshape(tile_rows, pair_count, key_count, features),
        value_terms.reshape(tile_rows, pair_count, key_count, features),
    )


def pass_keys(block, step):
    return from_behind(block, "tile", step)


def pass_terms(block, step):
    return from_behind(block, "tile", step)


def settle(received):
    rows_here = received.shape[-3]
    width_here = received.shape[-2]
    features = received.shape[-1]
    shaped = received.reshape(FRAMES, 4, rows_here, width_here, features).transpose(0, 2, 1, 3, 4)
    return shaped.reshape(FRAMES, 4 * rows_here, width_here, features)


def local(query_slab, key_slab, value_slab, upstream):
    query_rows, key_rows, value_rows = (
        lax.all_to_all(query_slab, "head", split_axis=3, concat_axis=2, tiled=True),
        lax.all_to_all(key_slab, "head", split_axis=3, concat_axis=2, tiled=True),
        lax.all_to_all(value_slab, "head", split_axis=3, concat_axis=2, tiled=True),
    )
    owner_count = lax.axis_size("tile")
    row_groups = owner_count // 4
    source_count = query_rows.shape[0]
    features = query_rows.shape[3]
    tile_rows = query_rows.shape[1] // row_groups
    tile_cols = FRAME_W // 16
    band_width = 4 * tile_cols
    line_count = 4 * tile_rows
    owner_index = lax.axis_index("tile")
    row_group = owner_index // 4
    col_group = owner_index % 4
    left_ok = col_group > 0
    right_ok = col_group < 3

    def to_owners(slab):
        shaped = slab.reshape(source_count, row_groups, tile_rows, 4, band_width, features)
        return shaped.transpose(1, 3, 0, 2, 4, 5).reshape(
            owner_count, source_count, tile_rows, band_width, features
        )

    query_got, key_got, value_got = (
        lax.all_to_all(to_owners(query_rows), "tile", split_axis=0, concat_axis=1, tiled=True),
        lax.all_to_all(to_owners(key_rows), "tile", split_axis=0, concat_axis=1, tiled=True),
        lax.all_to_all(to_owners(value_rows), "tile", split_axis=0, concat_axis=1, tiled=True),
    )
    owned_query = settle(query_got)
    owned_pair = jnp.stack((settle(key_got), settle(value_got)))
    from_left = pass_keys(owned_pair[:, :, :, band_width - 4 :], 1)
    from_right = pass_keys(owned_pair[:, :, :, 0:4], -1)
    from_left = jnp.where(left_ok, from_left, jnp.zeros_like(from_left))
    from_right = jnp.where(right_ok, from_right, jnp.zeros_like(from_right))
    wide_pair = jnp.concatenate((from_left, owned_pair, from_right), axis=3)
    from_above = pass_keys(wide_pair, 4)
    from_below = pass_keys(wide_pair, -4)
    nearby = jnp.concatenate((from_above, wide_pair, from_below), axis=2)
    query_tiles = to_tiles(owned_query, tile_rows, tile_cols)
    grad_tiles = to_tiles(
        upstream.reshape(FRAMES, line_count, band_width, features), tile_rows, tile_cols
    )
    usable = key_mask(
        tile_rows,
        tile_cols,
        row_group * tile_rows,
        col_group * tile_cols,
        row_groups * tile_rows,
        4 * tile_cols,
    )
    totals = jnp.zeros((2, FRAMES, line_count + 8, band_width + 8, features), jnp.float32)

    def one_column(totals, column):
        first_col = column * 4
        nearby_part = lax.dynamic_slice_in_dim(nearby, first_col, 12, 3)
        windows = window_keys(nearby_part, tile_rows, 1)
        query_part = lax.dynamic_slice_in_dim(query_tiles, column, 1, 1)
        grad_part = lax.dynamic_slice_in_dim(grad_tiles, column, 1, 1)
        usable_part = lax.dynamic_slice_in_dim(usable, column, 1, 1)
        mixed, query_grad, key_terms, value_terms = attend(
            query_part, windows[0], windows[1], grad_part, usable_part
        )
        folded = jnp.stack(
            (fold_keys(key_terms, tile_rows, 1), fold_keys(value_terms, tile_rows, 1))
        )
        current = lax.dynamic_slice_in_dim(totals, first_col, 12, 3)
        totals = lax.dynamic_update_slice_in_dim(totals, current + folded, first_col, 3)
        return (totals, (mixed[:, 0].astype(jnp.bfloat16), query_grad[:, 0].astype(jnp.bfloat16)))

    extended, (mixed, query_grad) = lax.scan(
        one_column, totals, jnp.arange(tile_cols, dtype=jnp.int32)
    )
    attended = from_tiles(jnp.swapaxes(mixed, 0, 1))
    query_out = from_tiles(jnp.swapaxes(query_grad, 0, 1))
    top_band = extended[:, :, 0:4].astype(jnp.bfloat16)
    bottom_band = extended[:, :, line_count + 4 :].astype(jnp.bfloat16)
    terms_below = pass_terms(top_band, -4).astype(jnp.float32)
    terms_above = pass_terms(bottom_band, 4).astype(jnp.float32)
    incoming = terms_above
    incoming = incoming + terms_below
    rowed = extended[:, :, 4 : line_count + 4] + incoming
    left_terms = rowed[:, :, :, 0:4].astype(jnp.bfloat16)
    right_terms = rowed[:, :, :, band_width + 4 :].astype(jnp.bfloat16)
    terms_right = pass_terms(left_terms, -1)
    terms_left = pass_terms(right_terms, 1)
    terms_right = jnp.where(right_ok, terms_right, jnp.zeros_like(terms_right)).astype(jnp.float32)
    terms_left = jnp.where(left_ok, terms_left, jnp.zeros_like(terms_left)).astype(jnp.float32)
    summed = rowed[:, :, :, 4 : band_width + 4]
    summed = summed + jnp.pad(terms_left, ((0, 0), (0, 0), (0, 0), (0, band_width - 4), (0, 0)))
    summed = summed + jnp.pad(terms_right, ((0, 0), (0, 0), (0, 0), (band_width - 4, 0), (0, 0)))
    summed = summed.astype(jnp.bfloat16)
    key_grad = summed[0].reshape(-1, features)
    value_grad = summed[1].reshape(-1, features)
    return (attended, query_out, key_grad, value_grad)


SLOTS = 14


def fast_kernel(query_hbm, key_hbm, value_hbm, grad_hbm, attended_ref, query_ref, key_ref, value_ref,
                slabs, grad_in, results, send_ref, up_ref, qkv, gbuf, obuf, acc, landed, rims,
                main_send, main_recv, ext_send, ext_recv, side_send, side_recv,
                up_send, up_recv, upx_send, upx_recv, out_send, out_recv, outx_send, outx_recv,
                rim_send, rim_recv, slab_sem, grad_sem, done_sem):
    tile = lax.axis_index("tile")
    head = lax.axis_index("head")
    me = tile * 4 + head
    row_half = tile // 4
    col = tile % 4

    def slab_copy(part, group):
        lanes_of = pl.ds(group * 10 * HEAD_DIM, 10 * HEAD_DIM)
        source = (query_hbm, key_hbm, value_hbm)[part]
        return pltpu.make_async_copy(source.at[:, :, :, lanes_of], slabs.at[part, :, :, :, lanes_of],
                                     slab_sem.at[part, group])

    def grad_copy(quarter):
        rows_of = pl.ds(64 * quarter, 64)
        return pltpu.make_async_copy(grad_hbm.at[rows_of], grad_in.at[rows_of], grad_sem.at[quarter])

    for group in range(4):
        for part in range(3):
            slab_copy(part, group).start()
    for quarter in range(4):
        grad_copy(quarter).start()

    barrier = pltpu.get_barrier_semaphore()

    def greet(step, carry):
        other = (me + step) % 32
        pl.semaphore_signal(barrier, inc=1, device_id=(other // 4, other % 4), device_id_type=MESH)
        return carry

    lax.fori_loop(1, 32, greet, 0)

    def regroup(first, second):
        upper = lax.broadcasted_iota(jnp.int32, first.shape, first.ndim - 2) < 4
        near = jnp.where(upper, first, pltpu.roll(second, 4, first.ndim - 2))
        far = jnp.where(upper, pltpu.roll(first, 4, first.ndim - 2), second)
        return near, far

    def lanes(which):
        return pl.ds(pl.multiple_of(which * HEAD_DIM, HEAD_DIM), HEAD_DIM)

    def prepare(which):
        for part in range(3):
            lines = slabs[part, :, :, :, lanes(which)].astype(jnp.float32).reshape(2, 2, 16, HEAD_DIM)
            first = lines[:, 0].reshape(4, 8, HEAD_DIM)
            second = lines[:, 1].reshape(4, 8, HEAD_DIM)
            for side, taken in enumerate(regroup(first, second)):
                ordered = jnp.stack((taken[0], taken[2], taken[1], taken[3])).reshape(32, HEAD_DIM)
                send_ref[which, part, side] = ordered.astype(jnp.bfloat16)

    def prepare_up(which):
        lines = grad_in[:, lanes(which)].astype(jnp.float32).reshape(16, 2, 8, HEAD_DIM)
        for side, taken in enumerate(regroup(lines[:, 0], lines[:, 1])):
            up_ref[which, side] = taken.reshape(FRAMES, 16, HEAD_DIM).astype(jnp.bfloat16)

    def prepare_shared(which, carry):
        prepare((which // 2) * 10 + 8 + which % 2)
        return carry

    for group in range(4):
        for part in range(3):
            slab_copy(part, group).wait()
    lax.fori_loop(0, 8, prepare_shared, 0)
    pl.semaphore_wait(barrier, 31)

    def push(src, dst, send_sem, recv_sem, to_tile, to_head):
        return pltpu.make_async_remote_copy(
            src_ref=src, dst_ref=dst, send_sem=send_sem, recv_sem=recv_sem,
            device_id=(to_tile, to_head), device_id_type=MESH)

    def landing(dst, recv_sem):
        return pltpu.make_async_copy(dst, dst, recv_sem)

    rows = pl.ds(16 * row_half, 16)

    def ext_parts(which):
        to_head, extra = which // 2, which % 2
        return to_head, extra, to_head * 10 + 8 + extra

    def ext_copy(which):
        to_head, extra, source = ext_parts(which)
        return push(send_ref.at[source], qkv.at[:, pl.ds(11, 2), tile],
                    ext_send.at[which], ext_recv.at[tile], 4 * extra + head, to_head)

    def ext_is_own(which):
        to_head, extra, source = ext_parts(which)
        return (4 * extra + head) * 4 + to_head == me

    def ext_start(which, carry):
        to_head, extra, source = ext_parts(which)

        @pl.when(ext_is_own(which))
        def _():
            pltpu.make_async_copy(send_ref.at[source], qkv.at[:, pl.ds(11, 2), tile], ext_recv.at[tile]).start()

        @pl.when(jnp.logical_not(ext_is_own(which)))
        def _():
            ext_copy(which).start()

        return carry

    lax.fori_loop(0, 8, ext_start, 0)

    def upx_copy(extra):
        return push(up_ref.at[8 + extra], gbuf.at[pl.ds(11, 2), :, rows],
                    upx_send.at[extra], upx_recv.at[row_half], 4 * extra + col, head)

    for quarter in range(4):
        grad_copy(quarter).wait()
    for extra in range(2):
        prepare_up(8 + extra)

        @pl.when(row_half == extra)
        def _(extra=extra):
            pltpu.make_async_copy(up_ref.at[8 + extra], gbuf.at[pl.ds(11, 2), :, rows],
                                  upx_recv.at[row_half]).start()

        @pl.when(row_half != extra)
        def _(extra=extra):
            upx_copy(extra).start()

    def up_copy(other):
        return push(up_ref.at[other], gbuf.at[pl.ds(1 + 2 * col, 2), :, rows],
                    up_send.at[other], up_recv.at[tile], other, head)

    def up_start(step, carry):
        other = (tile + 3 + step + step // 5) % 8
        prepare_up(other)
        up_copy(other).start()
        return carry

    lax.fori_loop(1, 8, up_start, 0)
    prepare_up(tile)
    pltpu.make_async_copy(up_ref.at[tile], gbuf.at[pl.ds(1 + 2 * col, 2), :, rows], up_recv.at[tile]).start()

    def main_copy(other):
        to_tile, to_head = other // 4, other % 4
        src = send_ref.at[to_head * 10 + to_tile]
        dst = qkv.at[:, pl.ds(1 + 2 * head, 2), tile]
        return push(src, dst, main_send.at[other], main_recv.at[me], to_tile, to_head)

    def main_peer(place):
        turn = place // 8
        column = (head + turn + turn // 2 - 2 * (turn // 3)) % 4
        other_tile = 4 * ((row_half + 1 - (place % 8) // 4) % 2) + column
        return other_tile * 4 + (head + place) % 4

    def main_start(place, carry):
        other = main_peer(place)
        prepare((other % 4) * 10 + other // 4)

        @pl.when(other != me)
        def _():
            main_copy(other).start()

        @pl.when(other == me)
        def _():
            pltpu.make_async_copy(send_ref.at[head * 10 + tile], qkv.at[:, pl.ds(1 + 2 * head, 2), tile],
                                  main_recv.at[me]).start()

        return carry

    lax.fori_loop(0, 16, main_start, 0)

    def ext_arrive(frame, carry):
        landing(qkv.at[:, pl.ds(11, 2), frame], ext_recv.at[frame]).wait()
        return carry

    lax.fori_loop(0, 8, ext_arrive, 0)

    def side_copy(side):
        source, target, step = ((12, 10, 1), (11, 13, -1))[side]
        return push(qkv.at[pl.ds(1, 2), source], qkv.at[pl.ds(1, 2), target],
                    side_send.at[side], side_recv.at[side], tile + step, head)

    @pl.when(col < 3)
    def _():
        side_copy(0).start()

    @pl.when(col > 0)
    def _():
        side_copy(1).start()

    lax.fori_loop(16, 32, main_start, 0)

    blank = jnp.zeros((FRAMES, 32, HEAD_DIM), jnp.bfloat16)
    for part in (1, 2):
        qkv[part, 0] = blank
        qkv[part, 9] = blank

        @pl.when(col == 0)
        def _(part=part):
            qkv[part, 10] = blank

        @pl.when(col == 3)
        def _(part=part):
            qkv[part, 13] = blank

    acc[...] = jnp.zeros_like(acc)

    scaling = HEAD_DIM ** (-0.5)
    key_at = lax.broadcasted_iota(jnp.int32, (768, 1), 0)

    def one_tile(job):
        first = job + 2 * (job // 8)
        low = jnp.where((job == 0) | ((job == 8) & (col == 0)), 256, 0)
        high = jnp.where((job == 7) | ((job == 9) & (col == 3)), 512, 768)
        usable = (key_at >= low) & (key_at < high)
        bias = jnp.where(usable, 0.0, -1e30)
        query = qkv[0, first + 1].reshape(256, HEAD_DIM)
        grad = gbuf[first + 1].reshape(256, HEAD_DIM)
        keys = qkv[1, pl.ds(first, 3)].reshape(768, HEAD_DIM)
        values = qkv[2, pl.ds(first, 3)].reshape(768, HEAD_DIM)
        scores = lax.dot_general(keys, query, (((1,), (1,)), ((), ())), preferred_element_type=jnp.float32)
        scores = scores * (scaling * math.log2(math.e)) + bias
        highest = jnp.max(scores, axis=0, keepdims=True)
        raised = jnp.exp2(scores - highest)
        weights = raised * (1.0 / jnp.sum(raised, axis=0, keepdims=True))
        weights_low = weights.astype(jnp.bfloat16)
        mixed = lax.dot_general(values, weights_low, (((0,), (0,)), ((), ())), preferred_element_type=jnp.float32)
        grad_across = grad.astype(jnp.float32).T
        offsets = jnp.sum(grad_across * mixed, axis=0, keepdims=True)
        weight_grad = lax.dot_general(values, grad, (((1,), (1,)), ((), ())), preferred_element_type=jnp.float32)
        score_low = (weights * (weight_grad - offsets)).astype(jnp.bfloat16)
        query_grad = lax.dot_general(keys, score_low, (((0,), (0,)), ((), ())), preferred_element_type=jnp.float32)
        obuf[0, first + 1] = mixed.T.astype(jnp.bfloat16).reshape(FRAMES, 32, HEAD_DIM)
        obuf[1, first + 1] = (query_grad * scaling).T.astype(jnp.bfloat16).reshape(FRAMES, 32, HEAD_DIM)
        key_terms = lax.dot_general(score_low, query, (((1,), (0,)), ((), ())), preferred_element_type=jnp.float32)
        value_terms = lax.dot_general(weights_low, grad, (((1,), (0,)), ((), ())), preferred_element_type=jnp.float32)
        acc[0, pl.ds(first, 3)] += (key_terms * scaling).reshape(3, 256, HEAD_DIM)
        acc[1, pl.ds(first, 3)] += value_terms.reshape(3, 256, HEAD_DIM)

    def settle(slot):
        for part in range(2):
            obuf[2 + part, slot] = acc[part, slot].astype(jnp.bfloat16).reshape(FRAMES, 32, HEAD_DIM)

    def out_piece(pair, other):
        return obuf.at[pl.ds(2 * pair, 2), pl.ds(1 + 2 * (other % 4), 2), :, pl.ds(16 * (other // 4), 16)]

    def out_copy(pair, other):
        return push(out_piece(pair, other), landed.at[pl.ds(2 * pair, 2), tile],
                    out_send.at[pair, other], out_recv.at[pair, tile], other, head)

    def out_start(pair, column):
        for step in (1, 0):
            other = 4 * ((row_half + step) % 2) + column

            @pl.when(other == tile)
            def _(other=other):
                pltpu.make_async_copy(out_piece(pair, other), landed.at[pl.ds(2 * pair, 2), tile],
                                      out_recv.at[pair, tile]).start()

            @pl.when(other != tile)
            def _(other=other):
                out_copy(pair, other).start()

    def outx_piece(pair, half):
        return obuf.at[pl.ds(2 * pair, 2), pl.ds(11, 2), :, pl.ds(16 * half, 16)]

    def outx_copy(pair, half):
        return push(outx_piece(pair, half), landed.at[pl.ds(2 * pair, 2), 8 + row_half],
                    outx_send.at[pair, half], outx_recv.at[pair, row_half], 4 * half + col, head)

    def outx_start(pair):
        for half in range(2):
            @pl.when(row_half == half)
            def _(half=half):
                pltpu.make_async_copy(outx_piece(pair, half), landed.at[pl.ds(2 * pair, 2), 8 + row_half],
                                      outx_recv.at[pair, row_half]).start()

            @pl.when(row_half != half)
            def _(half=half):
                outx_copy(pair, half).start()

    def rim_copy(side):
        slot, step = ((13, 1), (10, -1))[side]
        return push(obuf.at[pl.ds(2, 2), slot], rims.at[side], rim_send.at[side], rim_recv.at[side],
                    tile + step, head)

    @pl.when(col > 0)
    def _():
        landing(qkv.at[pl.ds(1, 2), 10], side_recv.at[0]).wait()

    @pl.when(col < 3)
    def _():
        landing(qkv.at[pl.ds(1, 2), 13], side_recv.at[1]).wait()

    for half in range(2):
        landing(gbuf.at[pl.ds(11, 2), :, pl.ds(16 * half, 16)], upx_recv.at[half]).wait()

    def ext_tile(job, carry):
        one_tile(job)
        return carry

    lax.fori_loop(8, 10, ext_tile, 0)
    settle(10)
    settle(13)

    @pl.when(col < 3)
    def _():
        rim_copy(0).start()

    @pl.when(col > 0)
    def _():
        rim_copy(1).start()

    outx_start(0)

    def finish_shared():
        @pl.when(col > 0)
        def _():
            landing(rims.at[0], rim_recv.at[0]).wait()
            for part in range(2):
                acc[part, 11] += rims[0, part].reshape(256, HEAD_DIM).astype(jnp.float32)

        @pl.when(col < 3)
        def _():
            landing(rims.at[1], rim_recv.at[1]).wait()
            for part in range(2):
                acc[part, 12] += rims[1, part].reshape(256, HEAD_DIM).astype(jnp.float32)

        settle(11)
        settle(12)
        outx_start(1)

    def main_arrive(place, carry):
        column = (col + 3 + place // 8) % 4
        frame = place % 8
        landing(qkv.at[:, pl.ds(1 + 2 * column, 2), frame], main_recv.at[frame * 4 + column]).wait()
        return carry

    lax.fori_loop(0, 24, main_arrive, 0)

    def up_arrive(other, carry):
        landing(gbuf.at[pl.ds(1 + 2 * (other % 4), 2), :, pl.ds(16 * (other // 4), 16)], up_recv.at[other]).wait()
        return carry

    lax.fori_loop(0, 8, up_arrive, 0)
    def settle_column(column):
        settle(1 + 2 * column)
        settle(2 + 2 * column)
        out_start(1, column)

    def main_tile(step, carry):
        @pl.when(step == 3)
        def _():
            lax.fori_loop(24, 32, main_arrive, 0)

        one_tile((step + 2 * col) % 8)

        @pl.when(step % 2 == 1)
        def _():
            out_start(0, (col + step // 2) % 4)

        @pl.when((step == 4) | (step == 6))
        def _():
            settle_column((col + step // 2 - 1) % 4)

        @pl.when(step == 3)
        def _():
            finish_shared()

        return carry

    lax.fori_loop(0, 8, main_tile, 0)
    settle_column((col + 3) % 4)
    settle_column(col)

    out_refs = (attended_ref, query_ref, key_ref, value_ref)

    def result_copy(part, which):
        return pltpu.make_async_copy(results.at[part, :, lanes(which)], out_refs[part].at[:, lanes(which)],
                                     done_sem.at[part, which])

    def place(part, which, near, far):
        even, odd = regroup(near.reshape(16, 8, HEAD_DIM), far.reshape(16, 8, HEAD_DIM))
        lines = jnp.stack((even, odd), axis=1).reshape(256, HEAD_DIM)
        results[part, :, lanes(which)] = lines.astype(jnp.bfloat16)
        result_copy(part, which).start()

    def wide(part, which, side):
        return landed[part, which, side].astype(jnp.float32)

    for pair in range(2):
        def out_arrive(step, carry, pair=pair):
            other = (tile + step) % 8
            landing(landed.at[pl.ds(2 * pair, 2), other], out_recv.at[pair, other]).wait()
            for part in (2 * pair, 2 * pair + 1):
                place(part, other, wide(part, other, 0), wide(part, other, 1))
            return carry

        lax.fori_loop(0, 8, out_arrive, 0)
        for extra in range(2):
            landing(landed.at[pl.ds(2 * pair, 2), 8 + extra], outx_recv.at[pair, extra]).wait()
            for part in (2 * pair, 2 * pair + 1):
                place(part, 8 + extra, wide(part, 8 + extra, 0), wide(part, 8 + extra, 1))

    def results_done(which, carry):
        for part in range(4):
            result_copy(part, which).wait()
        return carry

    lax.fori_loop(0, 10, results_done, 0)

    def main_left(step, carry):
        main_copy((me + step) % 32).wait_send()
        return carry

    lax.fori_loop(1, 32, main_left, 0)

    def group_left(step, carry):
        up_copy((tile + step) % 8).wait_send()
        out_copy(0, (tile + step) % 8).wait_send()
        out_copy(1, (tile + step) % 8).wait_send()
        return carry

    lax.fori_loop(1, 8, group_left, 0)

    def ext_left(which, carry):
        @pl.when(jnp.logical_not(ext_is_own(which)))
        def _():
            ext_copy(which).wait_send()

        return carry

    lax.fori_loop(0, 8, ext_left, 0)
    for half in range(2):
        @pl.when(row_half != half)
        def _(half=half):
            upx_copy(half).wait_send()
            outx_copy(0, half).wait_send()
            outx_copy(1, half).wait_send()

    @pl.when(col < 3)
    def _():
        side_copy(0).wait_send()
        rim_copy(0).wait_send()

    @pl.when(col > 0)
    def _():
        side_copy(1).wait_send()
        rim_copy(1).wait_send()


def fast_local(query_slab, key_slab, value_slab, upstream):
    dma = pltpu.SemaphoreType.DMA
    out = pl.pallas_call(
        fast_kernel,
        out_shape=[jax.ShapeDtypeStruct((256, 10 * HEAD_DIM), jnp.bfloat16)] * 4,
        in_specs=[pl.BlockSpec(memory_space=pltpu.HBM)] * 4,
        out_specs=[pl.BlockSpec(memory_space=pltpu.HBM)] * 4,
        scratch_shapes=[
            pltpu.VMEM((3, 4, 2, 8, 40 * HEAD_DIM), jnp.bfloat16),
            pltpu.VMEM((256, 10 * HEAD_DIM), jnp.bfloat16),
            pltpu.VMEM((4, 256, 10 * HEAD_DIM), jnp.bfloat16),
            pltpu.VMEM((40, 3, 2, 32, HEAD_DIM), jnp.bfloat16),
            pltpu.VMEM((10, 2, FRAMES, 16, HEAD_DIM), jnp.bfloat16),
            pltpu.VMEM((3, SLOTS, FRAMES, 32, HEAD_DIM), jnp.bfloat16),
            pltpu.VMEM((SLOTS, FRAMES, 32, HEAD_DIM), jnp.bfloat16),
            pltpu.VMEM((4, SLOTS, FRAMES, 32, HEAD_DIM), jnp.bfloat16),
            pltpu.VMEM((2, SLOTS, 256, HEAD_DIM), jnp.float32),
            pltpu.VMEM((4, 10, 2, FRAMES, 16, HEAD_DIM), jnp.bfloat16),
            pltpu.VMEM((2, 2, FRAMES, 32, HEAD_DIM), jnp.bfloat16),
            dma((32,)), dma((32,)), dma((8,)), dma((8,)), dma((2,)), dma((2,)),
            dma((8,)), dma((8,)), dma((2,)), dma((2,)), dma((2, 8)), dma((2, 8)), dma((2, 2)), dma((2, 2)),
            dma((2,)), dma((2,)), dma((3, 4)), dma((4,)), dma((4, 10)),
        ],
        compiler_params=pltpu.CompilerParams(
            collective_id=0, has_side_effects=True, vmem_limit_bytes=61 * 1024 * 1024
        ),
        cost_estimate=pl.CostEstimate(flops=3 * 10**9, bytes_accessed=8 * 10**6, transcendentals=2 * 10**6),
    )(query_slab, key_slab, value_slab, upstream)
    return tuple(out)


def solution(mesh):
    placed = (
        P("tile", None, "head", None),
        P("tile", None, "head", None),
        P("tile", None, "head", None),
        P("tile", "head"),
    )

    def chosen(query_slab, key_slab, value_slab, upstream):
        two_rows = query_slab.shape == (4, 2, 8, 40 * HEAD_DIM) and upstream.shape == (256, 10 * HEAD_DIM)
        body = fast_local if two_rows and mesh.shape["tile"] == 8 and mesh.shape["head"] == 4 else local
        return body(query_slab, key_slab, value_slab, upstream)

    return jax.shard_map(
        chosen,
        mesh=mesh,
        in_specs=placed,
        out_specs=(P("tile", "head"), P("tile", "head"), P("tile", "head"), P("tile", "head")),
        check_vma=False,
    )
```
